256 devices in a mesh: lat: 8 (over y, x_lo), lon: 32 (over x_hi, z, core).
Axes of the slice: x: 4 (x_hi: 2, x_lo: 2; x = x_hi * 2 + x_lo), y: 4, z: 8, core: 2. Of those that a mesh axis runs over, the one named last changes fastest.
Arguments:
- coarse_field: bfloat16 [1, 128, 256, 2048], P(None, None, 'lat', 'lon'), may hold values from -6 to 6
- cotangent: bfloat16 [1, 64, 512, 4096], P(None, None, 'lat', 'lon'), may hold values from -6 to 6
- tconv_weight: bfloat16 [4, 64, 128], replicated, may hold values from -0.5 to 0.5
- conv_weight: bfloat16 [64, 576], replicated, may hold values from -0.25 to 0.25
Outputs:
- coarse_grad: bfloat16 [1, 128, 256, 2048], P(None, None, 'lat', 'lon')
- tconv_grad: float32 [4, 64, 128], replicated
- conv_grad: float32 [64, 576], replicated
The draws below stay inside these ranges and needn't reach their ends.
All inputs are finite; a program needn't handle non-finite values.
Results may differ from the reference program's by a relative error of at most 0.0049.
Values may be sent and summed in bfloat16 or wider, within the bound.
A program may use at most 128 MiB of HBM per device.

```python
import math
import jax
import jax.numpy as jnp
from jax import lax

C_IN = 128
C2 = 64
NB = 1
NLAT = 512
NLON = 4096
HLAT = 256
HLON = 2048


def block_scale(own_key, shape, split, least, largest):
    gain, own = 1.0, jax.random.fold_in(own_key, 6)
    for position, shards_of in split:
        draws = jnp.exp(jax.random.uniform(jax.random.fold_in(own, position), (shards_of,), jnp.float32, least / len(split), largest / len(split)))
        gain = gain * jnp.repeat(draws, shape[position] // shards_of).reshape([-1 if axis == position else 1 for axis in range(len(shape))])
    return gain


def scatter_about(key, extent, deviation, reach, shards=(), kind=jnp.bfloat16):
    values = jax.random.normal(key, extent, jnp.float32) * deviation
    if len(shards) > 0:
        values = block_scale(key, extent, shards, -0.22, 0.18) * values
    return jnp.clip(values, min=-reach, max=reach).astype(kind)


def setup_inputs(seed: int = 0) -> dict:
    streams_of = jax.random.split(jax.random.key(seed), 5)
    coarse_field = scatter_about(streams_of[0], (NB, C_IN, HLAT, HLON), 1.0, 6.0, ((2, 8), (3, 32)))
    cotangent = scatter_about(streams_of[1], (NB, C2, NLAT, NLON), 1.0, 6.0, ((2, 8), (3, 32)))
    tconv_weight = scatter_about(streams_of[2], (4, C2, C_IN), C_IN ** -0.5, 0.5)
    conv_weight = scatter_about(streams_of[3], (C2, 9 * C2), (9 * C2) ** -0.5, 0.25)
    return dict(coarse_field=coarse_field, cotangent=cotangent, tconv_weight=tconv_weight, conv_weight=conv_weight)


OFFSETS = ((-1, -1), (-1, 0), (-1, 1), (0, -1), (0, 0), (0, 1), (1, -1), (1, 0), (1, 1))

def silu_slope(values):
    logistic = jax.nn.sigmoid(values)
    return logistic * (1.0 + values * (1.0 - logistic))

def extend_globe(field):
    opposite = field.shape[2] // 2
    top_row = jnp.roll(field[:, :1, :], -opposite, axis=2)
    bottom_row = jnp.roll(field[:, -1:, :], -opposite, axis=2)
    rows = jnp.concatenate([top_row, field, bottom_row], axis=1)
    return jnp.concatenate([rows[:, :, -1:], rows, rows[:, :, :1]], axis=2)

def reference(coarse_field, cotangent, tconv_weight, conv_weight):
    channels = conv_weight.shape[0]
    in_channels = tconv_weight.shape[2]
    rows_all = coarse_field.shape[2] * 2
    cols_all = coarse_field.shape[3] * 2
    scale = 1.0 / math.sqrt(coarse_field.shape[0] * rows_all * cols_all)
    tconv_taps = tconv_weight.astype(jnp.float32).reshape(2, 2, channels, in_channels)
    conv_taps = conv_weight.astype(jnp.float32).reshape(channels, 9, channels)

    def one_sample(carry, pair):
        coarse, grad_out = pair
        coarse32 = coarse.astype(jnp.float32)
        upsampled = jnp.einsum('pqck,kij->cipjq', tconv_taps, coarse32).reshape(channels, rows_all, cols_all)
        activated = (upsampled * jax.nn.sigmoid(upsampled)).astype(jnp.bfloat16)
        extended = extend_globe(activated).astype(jnp.float32)
        grad32 = grad_out.astype(jnp.float32)
        conv_terms = []
        scattered = jnp.zeros((channels, rows_all + 2, cols_all + 2), jnp.float32)
        for tap_index, (row_step, col_step) in enumerate(OFFSETS):
            window = extended[:, 1 + row_step:1 + row_step + rows_all, 1 + col_step:1 + col_step + cols_all]
            conv_terms.append(jnp.einsum('ors,crs->oc', grad32, window))
            part = jnp.einsum('oc,ors->crs', conv_taps[:, tap_index], grad32)
            scattered = scattered + jnp.pad(part, ((0, 0), (1 + row_step, 1 - row_step), (1 + col_step, 1 - col_step)))
        inner = scattered[:, :, 1:-1]
        inner = inner.at[:, :, -1].add(scattered[:, :, 0])
        inner = inner.at[:, :, 0].add(scattered[:, :, -1])
        opposite = cols_all // 2
        feature_grad = inner[:, 1:-1]
        feature_grad = feature_grad.at[:, 0].add(jnp.roll(inner[:, 0], opposite, axis=1))
        feature_grad = feature_grad.at[:, -1].add(jnp.roll(inner[:, -1], opposite, axis=1))
        pre_grad = (feature_grad * silu_slope(upsampled)).astype(jnp.bfloat16)
        blocks = pre_grad.astype(jnp.float32).reshape(channels, rows_all // 2, 2, cols_all // 2, 2)
        coarse_grad = jnp.einsum('pqck,cipjq->kij', tconv_taps, blocks).astype(jnp.bfloat16)
        tap_grad = jnp.einsum('cipjq,kij->pqck', blocks, coarse32).reshape(4, channels, in_channels)
        conv_sum = jnp.stack(conv_terms, axis=1).reshape(channels, 9 * channels)
        return ((carry[0] + tap_grad, carry[1] + conv_sum), coarse_grad)
    start = (jnp.zeros((4, channels, in_channels), jnp.float32), jnp.zeros((channels, 9 * channels), jnp.float32))
    totals, coarse_grads = lax.scan(one_sample, start, (coarse_field, cotangent))
    return (coarse_grads, totals[0] * scale, totals[1] * scale)
```

```python
import functools
import math

import jax
import jax.numpy as jnp
from jax import lax
from jax.experimental import pallas as pl
from jax.experimental.pallas import tpu as pltpu
from jax.sharding import PartitionSpec as P

MESH = pl.DeviceIdType.MESH
OFFSETS = ((-1, -1), (-1, 0), (-1, 1), (0, -1), (0, 0), (0, 1), (1, -1), (1, 0), (1, 1))


def shifted(array, axis, by):
    length = lax.axis_size(axis)
    return lax.ppermute(array, axis, [(i, (i + by) % length) for i in range(length)])


def with_halo(cells, sides, width, closed):
    for axis, dim in sides:
        count = lax.axis_size(axis)
        ends = count if closed else count - 1
        head = lax.slice_in_dim(cells, 0, width, axis=dim)
        tail = lax.slice_in_dim(cells, cells.shape[dim] - width, cells.shape[dim], axis=dim)
        cells = jnp.concatenate(
            [
                lax.ppermute(tail, axis, [(i, (i + 1) % count) for i in range(ends)]),
                cells,
                lax.ppermute(head, axis, [((i + 1) % count, i) for i in range(ends)]),
            ],
            axis=dim,
        )
    return cells


def silu_slope(values):
    logistic = jax.nn.sigmoid(values)
    return logistic * (1.0 + values * (1.0 - logistic))


def fix_poles(padded):
    lat_pos = lax.axis_index("lat")
    last_band = lax.axis_size("lat") - 1
    opposite = lax.axis_size("lon") // 2
    inner_rows = padded.shape[2] - 2
    at_north = lat_pos == 0
    outgoing = jnp.where(at_north, padded[:, :, 1], padded[:, :, inner_rows])
    incoming = shifted(outgoing, "lon", opposite)
    top_row = jnp.where(at_north, incoming, padded[:, :, 0])
    bottom_row = jnp.where(lat_pos == last_band, incoming, padded[:, :, inner_rows + 1])
    return jnp.concatenate(
        [top_row[:, :, None], padded[:, :, 1 : inner_rows + 1], bottom_row[:, :, None]], axis=2
    )


def extend(field):
    padded = with_halo(field, (("lat", 2),), 1, False)
    padded = fix_poles(padded)
    return with_halo(padded, (("lon", 3),), 1, True)


def return_rims(scattered):
    lat_pos = lax.axis_index("lat")
    last_band = lax.axis_size("lat") - 1
    opposite = lax.axis_size("lon") // 2
    inner = scattered[:, :, :, 1:-1]
    side_rims = jnp.concatenate([scattered[:, :, :, :1], scattered[:, :, :, -1:]], axis=3)
    arrived = with_halo(side_rims.astype(jnp.bfloat16), (("lon", 3),), 1, True).astype(
        side_rims.dtype
    )
    inner = jnp.concatenate(
        [
            inner[:, :, :, :1] + arrived[:, :, :, :1],
            inner[:, :, :, 1:-1],
            inner[:, :, :, -1:] + arrived[:, :, :, 3:],
        ],
        axis=3,
    )
    band_rims = jnp.concatenate([inner[:, :, :1], inner[:, :, -1:]], axis=2)
    landed = with_halo(band_rims.astype(jnp.bfloat16), (("lat", 2),), 1, False).astype(
        band_rims.dtype
    )
    core = inner[:, :, 1:-1]
    outgoing = jnp.where(lat_pos == 0, inner[:, :, 0], inner[:, :, -1])
    incoming = shifted(outgoing.astype(jnp.bfloat16), "lon", opposite).astype(outgoing.dtype)
    first_row = core[:, :, 0] + landed[:, :, 0] + jnp.where(lat_pos == 0, incoming, 0.0)
    final_row = core[:, :, -1] + landed[:, :, 3] + jnp.where(lat_pos == last_band, incoming, 0.0)
    return jnp.concatenate([first_row[:, :, None], core[:, :, 1:-1], final_row[:, :, None]], axis=2)


ROWS = 640
PART = 40


def sum_kernel(scale, x_ref, o_ref, seen, part, slots, done, a_send, a_recv, b_send, b_recv, c_send, c_recv, d_send, d_recv):
    lat, lon = lax.axis_index("lat"), lax.axis_index("lon")
    far, near = lon // 16, lon % 16
    mine = far * 8 + lat

    def plane(member):
        return {"lat": member % 8, "lon": (member // 8) * 16 + near}

    def line(member):
        return {"lat": lat, "lon": far * 16 + member}

    barrier = pltpu.get_barrier_semaphore()
    for d in range(1, 16):
        pl.semaphore_signal(barrier, inc=1, device_id=plane((mine + d) % 16), device_id_type=MESH)
        pl.semaphore_signal(barrier, inc=1, device_id=line((near + d) % 16), device_id_type=MESH)
    pl.semaphore_wait(barrier, 30)

    def rows_of(member):
        return pl.ds(pl.multiple_of(member * PART, 8), PART)

    firsts = []
    for d in range(1, 16):
        peer = (mine + d) % 16
        copy = pltpu.make_async_remote_copy(
            src_ref=x_ref.at[rows_of(peer)], dst_ref=seen.at[d], send_sem=a_send.at[d], recv_sem=a_recv.at[d],
            device_id=plane(peer), device_id_type=MESH)
        copy.start()
        firsts.append(copy)
    total = x_ref[rows_of(mine), :]
    for d in range(1, 16):
        firsts[d - 1].wait_recv()
        total = total + seen[d]
    part[...] = total

    for k in range(5):
        owner = 3 * k

        def send(k=k, owner=owner):
            pltpu.make_async_remote_copy(
                src_ref=part.at[pl.ds(8 * k, 8)], dst_ref=slots.at[near], send_sem=b_send.at[k], recv_sem=b_recv.at[near],
                device_id=line(owner), device_id_type=MESH).start()

        pl.when(near != owner)(send)
    for k in range(5):
        owner = 3 * k

        @pl.when(near == owner)
        def _(k=k, owner=owner):
            whole = part[8 * k:8 * k + 8, :]
            for m in range(16):
                if m != owner:
                    pltpu.make_async_remote_copy(
                        src_ref=part.at[pl.ds(8 * k, 8)], dst_ref=slots.at[m], send_sem=b_send.at[k],
                        recv_sem=b_recv.at[m], device_id=line(m), device_id_type=MESH).wait_recv()
                    whole = whole + slots[m]
            done[8 * k:8 * k + 8, :] = whole * scale
            for m in range(16):
                if m != owner:
                    pltpu.make_async_remote_copy(
                        src_ref=done.at[pl.ds(8 * k, 8)], dst_ref=done.at[pl.ds(8 * k, 8)], send_sem=c_send.at[m],
                        recv_sem=c_recv.at[k], device_id=line(m), device_id_type=MESH).start()
    for k in range(5):
        owner = 3 * k

        @pl.when(near != owner)
        def _(k=k, owner=owner):
            pltpu.make_async_remote_copy(
                src_ref=done.at[pl.ds(8 * k, 8)], dst_ref=done.at[pl.ds(8 * k, 8)], send_sem=c_send.at[0],
                recv_sem=c_recv.at[k], device_id=line(owner), device_id_type=MESH).wait_recv()

    lasts = []
    for d in range(1, 16):
        peer = (mine + d) % 16
        copy = pltpu.make_async_remote_copy(
            src_ref=done, dst_ref=o_ref.at[rows_of(mine)], send_sem=d_send.at[d], recv_sem=d_recv.at[d],
            device_id=plane(peer), device_id_type=MESH)
        copy.start()
        lasts.append(copy)
    o_ref[rows_of(mine), :] = done[...]

    for copy in firsts:
        copy.wait_send()
    for k in range(5):
        owner = 3 * k

        @pl.when(near != owner)
        def _(k=k, owner=owner):
            pltpu.make_async_remote_copy(
                src_ref=part.at[pl.ds(8 * k, 8)], dst_ref=slots.at[near], send_sem=b_send.at[k], recv_sem=b_recv.at[near],
                device_id=line(owner), device_id_type=MESH).wait_send()

        @pl.when(near == owner)
        def _(k=k, owner=owner):
            for m in range(16):
                if m != owner:
                    pltpu.make_async_remote_copy(
                        src_ref=done.at[pl.ds(8 * k, 8)], dst_ref=done.at[pl.ds(8 * k, 8)], send_sem=c_send.at[m],
                        recv_sem=c_recv.at[k], device_id=line(m), device_id_type=MESH).wait_send()
    for copy in lasts:
        copy.wait()


def summed(scale, values):
    dma = pltpu.SemaphoreType.DMA
    return pl.pallas_call(
        functools.partial(sum_kernel, scale),
        out_shape=jax.ShapeDtypeStruct((ROWS, 128), jnp.float32),
        in_specs=[pl.BlockSpec(memory_space=pltpu.VMEM)],
        out_specs=pl.BlockSpec(memory_space=pltpu.VMEM),
        scratch_shapes=[
            pltpu.VMEM((16, PART, 128), jnp.float32),
            pltpu.VMEM((PART, 128), jnp.float32),
            pltpu.VMEM((16, 8, 128), jnp.float32),
            pltpu.VMEM((PART, 128), jnp.float32),
            dma((16,)), dma((16,)), dma((8,)), dma((16,)), dma((16,)), dma((8,)), dma((16,)), dma((16,)),
        ],
        compiler_params=pltpu.CompilerParams(collective_id=1, has_side_effects=True),
        name="sums",
    )(values)


def per_device(coarse_field, cotangent, tconv_weight, conv_weight):
    batch, channels, rows_here, cols_here = cotangent.shape
    in_channels = coarse_field.shape[1]
    tconv_taps = tconv_weight.reshape(2, 2, channels, in_channels)
    conv_taps = conv_weight.reshape(channels, 9, channels)
    upsampled = jnp.einsum(
        "pqck,nkij->ncipjq", tconv_taps, coarse_field, preferred_element_type=jnp.float32
    )
    upsampled = upsampled.reshape(batch, channels, rows_here, cols_here)
    activated = (upsampled * jax.nn.sigmoid(upsampled)).astype(jnp.bfloat16)
    extended = extend(activated)
    conv_terms = []
    for tap_index, (row_step, col_step) in enumerate(OFFSETS):
        window = extended[
            :, :, 1 + row_step : 1 + row_step + rows_here, 1 + col_step : 1 + col_step + cols_here
        ]
        conv_terms.append(
            jnp.einsum("nors,ncrs->oc", cotangent, window, preferred_element_type=jnp.float32)
        )
    conv_grad = jnp.stack(conv_terms, axis=1).reshape(channels, 9 * channels)
    scattered = jnp.zeros((batch, channels, rows_here + 2, cols_here + 2), jnp.float32)
    for tap_index, (row_step, col_step) in enumerate(OFFSETS):
        part = jnp.einsum(
            "oc,nors->ncrs", conv_taps[:, tap_index], cotangent, preferred_element_type=jnp.float32
        )
        scattered = scattered + jnp.pad(
            part, ((0, 0), (0, 0), (1 + row_step, 1 - row_step), (1 + col_step, 1 - col_step))
        )
    feature_grad = return_rims(scattered)
    pre_grad = (feature_grad * silu_slope(upsampled)).astype(jnp.bfloat16)
    pre_blocks = pre_grad.reshape(batch, channels, rows_here // 2, 2, cols_here // 2, 2)
    coarse_grad = jnp.einsum(
        "pqck,ncipjq->nkij", tconv_taps, pre_blocks, preferred_element_type=jnp.float32
    ).astype(jnp.bfloat16)
    tconv_grad = jnp.einsum(
        "ncipjq,nkij->pqck", pre_blocks, coarse_field, preferred_element_type=jnp.float32
    )
    tconv_grad = tconv_grad.reshape(4, channels, in_channels)
    total_cells = batch * rows_here * cols_here * lax.axis_size("lat") * lax.axis_size("lon")
    scale = 1.0 / math.sqrt(total_cells)
    tiles = [conv_grad[:, 128 * m : 128 * m + 128] for m in range(4)]
    tiles.append(jnp.pad(conv_grad[:, 512:], ((0, 0), (0, 64))))
    values = jnp.concatenate(tiles + [tconv_grad.reshape(256, 128), jnp.zeros((64, 128), jnp.float32)])
    values = summed(scale, values)
    tiles = [values[64 * m : 64 * m + 64] for m in range(4)] + [values[256:320, :64]]
    return (coarse_grad, values[320:576].reshape(4, channels, in_channels), jnp.concatenate(tiles, axis=1))


def solution(mesh):
    return jax.shard_map(
        per_device,
        mesh=mesh,
        in_specs=(P(None, None, "lat", "lon"), P(None, None, "lat", "lon"), P(), P()),
        out_specs=(P(None, None, "lat", "lon"), P(), P()),
        check_vma=False,
    )
```

```python
import functools
import math

import jax
import jax.numpy as jnp
from jax import lax
from jax.experimental import pallas as pl
from jax.experimental.pallas import tpu as pltpu
from jax.sharding import PartitionSpec as P

MESH = pl.DeviceIdType.MESH
F32, BF16 = jnp.float32, jnp.bfloat16
OWN, BESIDE = 0, 1


def row_step(source, half, p):
    step = p - half if source == OWN else (p - 2 if half == 0 else p + 1)
    return step if abs(step) <= 1 else None


def col_step(window, q):
    step = (q, q - 1, q + 1, q - 2)[window]
    return step if abs(step) <= 1 else None


def window_blocks():
    for source in (OWN, BESIDE):
        for window in range(4):
            for half in range(2):
                for p in range(2):
                    for q in range(2):
                        a, b = row_step(source, half, p), col_step(window, q)
                        if a is not None and b is not None:
                            yield source, window, half, p, q, 3 * (a + 1) + b + 1


def pole_blocks():
    for window in range(4):
        for half in range(2):
            for q in range(2):
                b = col_step(window, q)
                if b is not None:
                    yield window, half, half, q, 3 * (2 * half) + b + 1


def across(a, b):
    return lax.dot_general(a, b, (((1,), (1,)), ((), ())), preferred_element_type=F32)


def times(a, b):
    return jnp.dot(a, b, preferred_element_type=F32)


def section_kernel(
    coarse_ref, cot_ref, tconv_ref, conv_ref, out_ref, sums_ref,
    spread, tiles, west_out, east_out, west_in, east_in, patches, act_t, slope, pre_t, weights, pole_weights,
    pole_patches, pole_extra, pole_sums, send_sem, recv_sem,
):
    pairs = coarse_ref.shape[0] // 64
    chunks = pairs // 4
    lat, lon = lax.axis_index("lat"), lax.axis_index("lon")
    lats, lons = lax.axis_size("lat"), lax.axis_size("lon")
    at_north, at_south = lat == 0, lat == lats - 1
    opposite = lax.rem(lon + lons // 2, lons)
    up_lat, up_lon = jnp.where(at_north, 0, lat - 1), jnp.where(at_north, opposite, lon)
    down_lat, down_lon = jnp.where(at_south, lats - 1, lat + 1), jnp.where(at_south, opposite, lon)

    def beside(which_lat, which_lon, by):
        return {"lat": which_lat, "lon": lax.rem(which_lon + by + lons, lons)}

    barrier = pltpu.get_barrier_semaphore()
    for which in ((lat, lon, -1), (lat, lon, 1), (up_lat, up_lon, -1), (up_lat, up_lon, 0), (up_lat, up_lon, 1),
                  (down_lat, down_lon, -1), (down_lat, down_lon, 0), (down_lat, down_lon, 1)):
        pl.semaphore_signal(barrier, inc=1, device_id=beside(*which), device_id_type=MESH)

    rows, cols = lax.broadcasted_iota(jnp.int32, (128, 128), 0), lax.broadcasted_iota(jnp.int32, (128, 128), 1)
    order = jnp.where(rows == (cols % 64) * 2 + cols // 64, 1.0, 0.0).astype(BF16)
    height = 2 * pairs

    def reorder(n, carry):
        at = pl.ds(pl.multiple_of(n * 512, 512), 512)
        spread[at, :] = times(cot_ref[at, :], order)
        return carry

    lax.fori_loop(0, 64 * height // 512, reorder, 0)

    def make_tile(i, carry):
        pair = jnp.concatenate(
            [spread[pl.ds(2 * i, 64, stride=height), :], spread[pl.ds(2 * i + 1, 64, stride=height), :]], axis=0)
        tile = pair.T
        tiles[i + 1, 0] = tile[:64].astype(BF16)
        tiles[i + 1, 1] = tile[64:].astype(BF16)
        west_out[pl.ds(i, 1), :] = tile[:1]
        east_out[pl.ds(i, 1), :] = tile[127:]
        return carry

    lax.fori_loop(0, pairs, make_tile, 0, unroll=2)

    pl.semaphore_wait(barrier, 8)
    copies = []

    def send(source, target, sem, which, landed):
        copy = pltpu.make_async_remote_copy(
            src_ref=source, dst_ref=target, send_sem=send_sem.at[sem], recv_sem=recv_sem.at[landed],
            device_id=beside(*which), device_id_type=MESH)
        copy.start()
        copies.append(copy)

    head, tail = pl.ds(0, 8), pl.ds(pairs - 8, 8)
    up_slot = jnp.where(at_north, 0, pairs + 1)
    down_slot = jnp.where(at_south, pairs + 1, 0)
    up_corner = pl.ds(pl.multiple_of(jnp.where(at_north, 0, pairs + 8), 8), 8)
    down_corner = pl.ds(pl.multiple_of(jnp.where(at_south, pairs + 8, 0), 8), 8)
    up_sem, down_sem = jnp.where(at_north, 0, 1), jnp.where(at_south, 1, 0)
    send(west_out, east_in.at[pl.ds(8, pairs)], 0, (lat, lon, -1), 6)
    send(east_out, west_in.at[pl.ds(8, pairs)], 1, (lat, lon, 1), 7)
    send(tiles.at[1, pl.ds(0, 2)], tiles.at[up_slot, pl.ds(0, 2)], 2, (up_lat, up_lon, 0), up_sem)
    send(tiles.at[pairs, pl.ds(0, 2)], tiles.at[down_slot, pl.ds(0, 2)], 3, (down_lat, down_lon, 0), down_sem)
    send(west_out.at[head], east_in.at[up_corner], 4, (up_lat, up_lon, -1), 2 + up_sem)
    send(east_out.at[head], west_in.at[up_corner], 5, (up_lat, up_lon, 1), 4 + up_sem)
    send(west_out.at[tail], east_in.at[down_corner], 6, (down_lat, down_lon, -1), 2 + down_sem)
    send(east_out.at[tail], west_in.at[down_corner], 7, (down_lat, down_lon, 1), 4 + down_sem)

    def activate(n, carry):
        at = pl.ds(pl.multiple_of(n * 256, 256), 256)
        up = across(coarse_ref[at, :], tconv_ref[...])
        logistic = 0.5 * jnp.tanh(0.5 * up) + 0.5
        act_t[:, at] = (up * logistic).astype(BF16).T
        slope[at, :] = logistic * (1.0 + up * (1.0 - logistic))
        return carry

    lax.fori_loop(0, chunks, activate, 0)

    def block(tap):
        return conv_ref[:, 64 * tap : 64 * tap + 64]

    none = jnp.zeros((64, 64), BF16)
    places = {(s, w, h, p, q): t for s, w, h, p, q, t in window_blocks()}
    for s, w, h in [(s, w, h) for s in range(2) for w in range(4) for h in range(2)]:
        line = [block(places[s, w, h, p, q]) if (s, w, h, p, q) in places else none for p in range(2) for q in range(2)]
        at = w * 256 + s * 128 + h * 64
        weights[at : at + 64, :] = jnp.concatenate(line, axis=1)
    places = {(w, h, p, q): t for w, h, p, q, t in pole_blocks()}
    for w, h in [(w, h) for w in range(4) for h in range(2)]:
        line = [block(places[w, h, p, q]) if (w, h, p, q) in places else none for p in range(2) for q in range(2)]
        at = w * 128 + h * 64
        pole_weights[at : at + 64, :] = jnp.concatenate(line, axis=1)

    pole_extra[...] = jnp.zeros_like(pole_extra)
    pole_sums[...] = jnp.zeros_like(pole_sums)

    for landed, source in enumerate(
        (tiles.at[0, pl.ds(0, 2)], tiles.at[0, pl.ds(0, 2)], east_in.at[head], east_in.at[head], west_in.at[head],
         west_in.at[head], east_in.at[pl.ds(8, pairs)], west_in.at[pl.ds(8, pairs)])):
        pltpu.make_async_remote_copy(
            src_ref=source, dst_ref=source, send_sem=send_sem.at[0], recv_sem=recv_sem.at[landed],
            device_id=beside(lat, lon, 1), device_id_type=MESH).wait_recv()

    line = lax.broadcasted_iota(jnp.int32, (64, 128), 0)

    def shift(i, west_row, east_row):
        even, odd = tiles[i, 0].astype(F32), tiles[i, 1].astype(F32)
        tiles[i, 2] = jnp.where(line == 0, west_in[pl.ds(west_row, 1), :], pltpu.roll(odd, 1, 0)).astype(BF16)
        tiles[i, 3] = jnp.where(line == 63, east_in[pl.ds(east_row, 1), :], pltpu.roll(even, 63, 0)).astype(BF16)

    def shift_own(i, carry):
        shift(i, i + 7, i + 7)
        return carry

    north_row, south_row = jnp.where(at_north, 0, 7), jnp.where(at_south, pairs + 15, pairs + 8)
    shift(0, north_row, north_row)
    shift(pairs + 1, south_row, south_row)
    lax.fori_loop(1, pairs + 1, shift_own, 0, unroll=2)

    lane = lax.broadcasted_iota(jnp.int32, (64, 128), 1)
    blank = jnp.zeros((64, 128), BF16)

    def take_pole(slot, first, keep):
        for w in range(4):
            pole_patches[first : first + 64, 128 * w : 128 * w + 128] = jnp.where(keep, tiles[slot, w].astype(F32), 0.0).astype(BF16)
            pole_patches[64 - first : 128 - first, 128 * w : 128 * w + 128] = blank
            tiles[slot, w] = blank

    last = pairs * 64

    @pl.when(at_north)
    def _():
        take_pole(0, 0, lane < 64)
        pole_extra[0] = times(pole_patches[...], pole_weights[...])
        pole_sums[...] = times(act_t[:, :128], pole_patches[...])

    @pl.when(at_south)
    def _():
        take_pole(pairs + 1, 64, lane >= 64)
        pole_extra[1] = times(pole_patches[...], pole_weights[...])
        pole_sums[...] = times(act_t[:, last - 128 :], pole_patches[...])

    def lay(i, carry):
        at = pl.ds(pl.multiple_of(i * 64, 64), 64)
        for w in range(4):
            patches[at, 256 * w : 256 * w + 128] = tiles[i + 1, w]
            patches[at, 256 * w + 128 : 256 * w + 256] = jnp.where(lane < 64, tiles[i + 2, w], tiles[i, w])
        return carry

    lax.fori_loop(0, pairs, lay, 0, unroll=2)

    found = {}

    def add(tap, value):
        found[tap] = value if tap not in found else found[tap] + value

    for w in range(4):
        grads = times(act_t[...], patches[:, 256 * w : 256 * w + 256])
        for s, ww, h, p, q, t in window_blocks():
            if ww == w:
                at, col = 128 * p + 64 * q, s * 128 + h * 64
                add(t, grads[at : at + 64, col : col + 64])
    for w, h, p, q, t in pole_blocks():
        at, col = 128 * p + 64 * q, w * 128 + h * 64
        add(t, pole_sums[at : at + 64, col : col + 64])
    for m in range(5):
        both = jnp.concatenate([found[2 * m], found[2 * m + 1] if m < 4 else jnp.zeros((64, 64), F32)], axis=0)
        sums_ref[64 * m : 64 * m + 64, :] = both.T

    for n in range(chunks):
        at = slice(n * 256, n * 256 + 256)
        grad = times(patches[at, :], weights[...])
        if n == 0:
            grad = jnp.concatenate([grad[:128] + pole_extra[0], grad[128:]], axis=0)
        if n == chunks - 1:
            grad = jnp.concatenate([grad[:128], grad[128:] + pole_extra[1]], axis=0)
        pre = (grad * slope[at, :]).astype(BF16)
        pre_t[:, at] = pre.T
        out_ref[at, :] = times(pre, tconv_ref[...]).astype(BF16)
    sums_ref[320:576, :] = times(pre_t[...], coarse_ref[...])
    sums_ref[576:, :] = jnp.zeros((64, 128), F32)

    for copy in copies:
        copy.wait_send()


def section(coarse, cotangent, tconv, conv):
    cells = coarse.shape[0]
    pairs = cells // 64
    vmem = pl.BlockSpec(memory_space=pltpu.VMEM)
    return pl.pallas_call(
        section_kernel,
        out_shape=(jax.ShapeDtypeStruct((cells, 128), BF16), jax.ShapeDtypeStruct((ROWS, 128), F32)),
        in_specs=[vmem] * 4,
        out_specs=(vmem, vmem),
        scratch_shapes=[
            pltpu.VMEM((cells * 2, 128), F32),
            pltpu.VMEM((pairs + 2, 4, 64, 128), BF16),
            pltpu.VMEM((pairs, 128), F32), pltpu.VMEM((pairs, 128), F32),
            pltpu.VMEM((pairs + 16, 128), F32), pltpu.VMEM((pairs + 16, 128), F32),
            pltpu.VMEM((cells, 1024), BF16),
            pltpu.VMEM((256, cells), BF16),
            pltpu.VMEM((cells, 256), F32),
            pltpu.VMEM((256, cells), BF16),
            pltpu.VMEM((1024, 256), BF16),
            pltpu.VMEM((512, 256), BF16),
            pltpu.VMEM((128, 512), BF16),
            pltpu.VMEM((2, 128, 256), F32),
            pltpu.VMEM((256, 512), F32),
            pltpu.SemaphoreType.DMA((8,)), pltpu.SemaphoreType.DMA((8,)),
        ],
        compiler_params=pltpu.CompilerParams(collective_id=0, has_side_effects=True, vmem_limit_bytes=40 * 2**20),
        name="section",
    )(coarse, cotangent, tconv, conv)


ROWS = 640
PART = 40


def sum_kernel(scale, x_ref, o_ref, seen, part, slots, done, a_send, a_recv, b_send, b_recv, c_send, c_recv, d_send, d_recv):
    lat, lon = lax.axis_index("lat"), lax.axis_index("lon")
    far, near = lon // 16, lon % 16
    mine = far * 8 + lat

    def plane(member):
        return {"lat": member % 8, "lon": (member // 8) * 16 + near}

    def line(member):
        return {"lat": lat, "lon": far * 16 + member}

    barrier = pltpu.get_barrier_semaphore()
    for d in range(1, 16):
        pl.semaphore_signal(barrier, inc=1, device_id=plane((mine + d) % 16), device_id_type=MESH)
        pl.semaphore_signal(barrier, inc=1, device_id=line((near + d) % 16), device_id_type=MESH)
    pl.semaphore_wait(barrier, 30)

    def rows_of(member):
        return pl.ds(pl.multiple_of(member * PART, 8), PART)

    firsts = []
    for d in range(1, 16):
        peer = (mine + d) % 16
        copy = pltpu.make_async_remote_copy(
            src_ref=x_ref.at[rows_of(peer)], dst_ref=seen.at[d], send_sem=a_send.at[d], recv_sem=a_recv.at[d],
            device_id=plane(peer), device_id_type=MESH)
        copy.start()
        firsts.append(copy)
    total = x_ref[rows_of(mine), :]
    for d in range(1, 16):
        firsts[d - 1].wait_recv()
        total = total + seen[d]
    part[...] = total

    for k in range(5):
        owner = 3 * k

        def send(k=k, owner=owner):
            pltpu.make_async_remote_copy(
                src_ref=part.at[pl.ds(8 * k, 8)], dst_ref=slots.at[near], send_sem=b_send.at[k], recv_sem=b_recv.at[near],
                device_id=line(owner), device_id_type=MESH).start()

        pl.when(near != owner)(send)
    for k in range(5):
        owner = 3 * k

        @pl.when(near == owner)
        def _(k=k, owner=owner):
            whole = part[8 * k:8 * k + 8, :]
            for m in range(16):
                if m != owner:
                    pltpu.make_async_remote_copy(
                        src_ref=part.at[pl.ds(8 * k, 8)], dst_ref=slots.at[m], send_sem=b_send.at[k],
                        recv_sem=b_recv.at[m], device_id=line(m), device_id_type=MESH).wait_recv()
                    whole = whole + slots[m]
            done[8 * k:8 * k + 8, :] = whole * scale
            for m in range(16):
                if m != owner:
                    pltpu.make_async_remote_copy(
                        src_ref=done.at[pl.ds(8 * k, 8)], dst_ref=done.at[pl.ds(8 * k, 8)], send_sem=c_send.at[m],
                        recv_sem=c_recv.at[k], device_id=line(m), device_id_type=MESH).start()
    for k in range(5):
        owner = 3 * k

        @pl.when(near != owner)
        def _(k=k, owner=owner):
            pltpu.make_async_remote_copy(
                src_ref=done.at[pl.ds(8 * k, 8)], dst_ref=done.at[pl.ds(8 * k, 8)], send_sem=c_send.at[0],
                recv_sem=c_recv.at[k], device_id=line(owner), device_id_type=MESH).wait_recv()

    lasts = []
    for d in range(1, 16):
        peer = (mine + d) % 16
        copy = pltpu.make_async_remote_copy(
            src_ref=done, dst_ref=o_ref.at[rows_of(mine)], send_sem=d_send.at[d], recv_sem=d_recv.at[d],
            device_id=plane(peer), device_id_type=MESH)
        copy.start()
        lasts.append(copy)
    o_ref[rows_of(mine), :] = done[...]

    for copy in firsts:
        copy.wait_send()
    for k in range(5):
        owner = 3 * k

        @pl.when(near != owner)
        def _(k=k, owner=owner):
            pltpu.make_async_remote_copy(
                src_ref=part.at[pl.ds(8 * k, 8)], dst_ref=slots.at[near], send_sem=b_send.at[k], recv_sem=b_recv.at[near],
                device_id=line(owner), device_id_type=MESH).wait_send()

        @pl.when(near == owner)
        def _(k=k, owner=owner):
            for m in range(16):
                if m != owner:
                    pltpu.make_async_remote_copy(
                        src_ref=done.at[pl.ds(8 * k, 8)], dst_ref=done.at[pl.ds(8 * k, 8)], send_sem=c_send.at[m],
                        recv_sem=c_recv.at[k], device_id=line(m), device_id_type=MESH).wait_send()
    for copy in lasts:
        copy.wait()


def summed(scale, values):
    dma = pltpu.SemaphoreType.DMA
    return pl.pallas_call(
        functools.partial(sum_kernel, scale),
        out_shape=jax.ShapeDtypeStruct((ROWS, 128), jnp.float32),
        in_specs=[pl.BlockSpec(memory_space=pltpu.VMEM)],
        out_specs=pl.BlockSpec(memory_space=pltpu.VMEM),
        scratch_shapes=[
            pltpu.VMEM((16, PART, 128), jnp.float32),
            pltpu.VMEM((PART, 128), jnp.float32),
            pltpu.VMEM((16, 8, 128), jnp.float32),
            pltpu.VMEM((PART, 128), jnp.float32),
            dma((16,)), dma((16,)), dma((8,)), dma((16,)), dma((16,)), dma((8,)), dma((16,)), dma((16,)),
        ],
        compiler_params=pltpu.CompilerParams(collective_id=1, has_side_effects=True),
        name="sums",
    )(values)


def per_device(coarse_field, cotangent, tconv_weight, conv_weight):
    batch, channels, rows_here, cols_here = cotangent.shape
    in_channels = coarse_field.shape[1]
    coarse = coarse_field.transpose(0, 2, 3, 1).reshape(-1, in_channels)
    coarse_grad, sums = section(
        coarse, cotangent.reshape(channels * rows_here, cols_here), tconv_weight.reshape(4 * channels, in_channels),
        conv_weight)
    total_cells = batch * rows_here * cols_here * lax.axis_size("lat") * lax.axis_size("lon")
    sums = summed(1.0 / math.sqrt(total_cells), sums)
    tiles = [sums[64 * m : 64 * m + 64] for m in range(4)] + [sums[256:320, :64]]
    coarse_grad = coarse_grad.reshape(batch, rows_here // 2, cols_here // 2, in_channels).transpose(0, 3, 1, 2)
    return coarse_grad, sums[320:576].reshape(4, channels, in_channels), jnp.concatenate(tiles, axis=1)


def solution(mesh):
    return jax.shard_map(
        per_device,
        mesh=mesh,
        in_specs=(P(None, None, "lat", "lon"), P(None, None, "lat", "lon"), P(), P()),
        out_specs=(P(None, None, "lat", "lon"), P(), P()),
        check_vma=False,
    )
```

```python
import functools
import math

import jax
import jax.numpy as jnp
from jax import lax
from jax.experimental import pallas as pl
from jax.experimental.pallas import tpu as pltpu
from jax.sharding import PartitionSpec as P

MESH = pl.DeviceIdType.MESH
F32, BF16 = jnp.float32, jnp.bfloat16
OWN, BESIDE = 0, 1
VMEM_LIMIT = 62 * 2**20


def row_step(source, half, p):
    step = p - half if source == OWN else (p - 2 if half == 0 else p + 1)
    return step if abs(step) <= 1 else None


def col_step(window, q):
    step = (q, q - 1, q + 1, q - 2)[window]
    return step if abs(step) <= 1 else None


def window_blocks():
    for source in (OWN, BESIDE):
        for window in range(4):
            for half in range(2):
                for p in range(2):
                    for q in range(2):
                        a, b = row_step(source, half, p), col_step(window, q)
                        if a is not None and b is not None:
                            yield source, window, half, p, q, 3 * (a + 1) + b + 1


def pole_blocks():
    for window in range(4):
        for half in range(2):
            for q in range(2):
                b = col_step(window, q)
                if b is not None:
                    yield window, half, half, q, 3 * (2 * half) + b + 1


def across(a, b):
    return lax.dot_general(a, b, (((1,), (1,)), ((), ())), preferred_element_type=F32)


def times(a, b):
    return jnp.dot(a, b, preferred_element_type=F32)


class Sum:
    def __init__(self, source, half, arrived, seen, along, final, scale, send, recv):
        self.source, self.half, self.arrived, self.seen, self.along, self.final = source, half, arrived, seen, along, final
        self.scale, self.send, self.recv = scale, send, recv
        self.lat, lon = lax.axis_index("lat"), lax.axis_index("lon")
        self.lats, lons = lax.axis_size("lat"), lax.axis_size("lon")
        self.side = lons // 2
        self.members, self.length = 2 * self.lats, lons // 4
        self.far = jnp.where(lon >= self.side, 1, 0)
        self.near = lon - self.far * self.side
        self.z, self.core = self.near // 2, self.near % 2
        self.mine = self.far * self.lats + self.lat

    def other(self):
        return {"lat": self.lat, "lon": self.far * self.side + self.z * 2 + 1 - self.core}

    def member(self, d):
        flip, by = d // self.lats, d % self.lats
        lat = self.lat + by
        lat = jnp.where(lat >= self.lats, lat - self.lats, lat)
        return lat, (1 - self.far if flip else self.far)

    def plane(self, d):
        lat, far = self.member(d)
        return {"lat": lat, "lon": far * self.side + self.near}

    def line(self, e):
        z = self.z + e
        z = jnp.where(z >= self.length, z - self.length, z)
        return {"lat": self.lat, "lon": self.far * self.side + z * 2 + self.core}

    def copy(self, source, target, phase, where):
        return pltpu.make_async_remote_copy(
            src_ref=source, dst_ref=target, send_sem=self.send.at[phase], recv_sem=self.recv.at[phase], device_id=where,
            device_id_type=MESH)

    def greet(self, barrier):
        peers = [self.other()] + [self.plane(d) for d in range(1, self.members)]
        peers += [self.line(e) for e in range(1, self.length)]
        for peer in peers:
            pl.semaphore_signal(barrier, inc=1, device_id=peer, device_id_type=MESH)
        return len(peers)

    def all_of(self, phase):
        part = (self.arrived, self.seen.at[pl.ds(1, self.members - 1)], self.along.at[pl.ds(1, self.length - 1)],
                self.seen.at[pl.ds(1, self.members - 1)], self.arrived)[phase]
        return self.copy(part, part, phase, self.other())

    def start(self):
        self.copy(self.source.at[1 - self.core], self.arrived, 0, self.other()).start()

    def scatter(self):
        self.all_of(0).wait_recv()
        self.half[...] = self.source[self.core] + self.arrived[...]
        for d in range(1, self.members):
            lat, far = self.member(d)
            self.copy(self.half.at[far * self.lats + lat], self.seen.at[d], 1, self.plane(d)).start()

    def pass_on(self):
        self.all_of(1).wait_recv()
        total = self.half[self.mine]
        for d in range(1, self.members):
            total = total + self.seen[d]
        self.along[self.z] = total
        for e in range(1, self.length):
            self.copy(self.along.at[self.z], self.along.at[self.z], 2, self.line(e)).start()

    def give_back(self):
        self.all_of(2).wait_recv()
        total = self.along[0]
        for z in range(1, self.length):
            total = total + self.along[z]
        self.final[self.core, self.mine] = total * self.scale
        for d in range(1, self.members):
            at = self.final.at[self.core, self.mine]
            self.copy(at, at, 3, self.plane(d)).start()

    def bring_home(self):
        self.all_of(3).wait_recv()
        self.copy(self.final.at[self.core], self.final.at[self.core], 4, self.other()).start()

    def end(self):
        self.all_of(4).wait_recv()
        for phase in range(5):
            self.all_of(phase).wait_send()


def section_kernel(
    scale, coarse_hbm, cot_hbm, tconv_hbm, conv_hbm, out_ref, taps_out, conv_out,
    coarse_ref, cot_ref, tconv_ref, conv_ref,
    spread, tiles, west_out, east_out, west_in, east_in, patches, act_t, slope, pre, pre_t, weights, pole_weights,
    pole_patches, pole_extra, pole_sums, send_sem, recv_sem, load_sem,
    shares, half, arrived, seen, along, final, sum_send, sum_recv,
):
    pairs = coarse_ref.shape[0] // 64
    chunks = pairs // 4
    loads = []
    quarter = cot_ref.shape[0] // 4
    for n in range(4):
        at = pl.ds(n * quarter, quarter)
        loads.append(pltpu.make_async_copy(cot_hbm.at[at], cot_ref.at[at], load_sem.at[n]))
    for n, (source, target) in enumerate(((coarse_hbm, coarse_ref), (tconv_hbm, tconv_ref), (conv_hbm, conv_ref))):
        loads.append(pltpu.make_async_copy(source, target, load_sem.at[4 + n]))
    for load in loads:
        load.start()

    lat, lon = lax.axis_index("lat"), lax.axis_index("lon")
    lats, lons = lax.axis_size("lat"), lax.axis_size("lon")
    at_north, at_south = lat == 0, lat == lats - 1
    opposite = lax.rem(lon + lons // 2, lons)
    up_lat, up_lon = jnp.where(at_north, 0, lat - 1), jnp.where(at_north, opposite, lon)
    down_lat, down_lon = jnp.where(at_south, lats - 1, lat + 1), jnp.where(at_south, opposite, lon)

    def beside(which_lat, which_lon, by):
        return {"lat": which_lat, "lon": lax.rem(which_lon + by + lons, lons)}

    total = Sum(shares, half, arrived, seen, along, final, scale, sum_send, sum_recv)

    barrier = pltpu.get_barrier_semaphore()
    greeted = 8 + total.greet(barrier)
    for which in ((lat, lon, -1), (lat, lon, 1), (up_lat, up_lon, -1), (up_lat, up_lon, 0), (up_lat, up_lon, 1),
                  (down_lat, down_lon, -1), (down_lat, down_lon, 0), (down_lat, down_lon, 1)):
        pl.semaphore_signal(barrier, inc=1, device_id=beside(*which), device_id_type=MESH)

    rows, cols = lax.broadcasted_iota(jnp.int32, (128, 128), 0), lax.broadcasted_iota(jnp.int32, (128, 128), 1)
    order = jnp.where(rows == (cols % 64) * 2 + cols // 64, 1.0, 0.0).astype(BF16)
    height = 2 * pairs

    def reorder(n, carry):
        at = pl.ds(pl.multiple_of(n * 512, 512), 512)
        spread[at, :] = times(cot_ref[at, :], order)
        return carry

    for n in range(4):
        loads[n].wait()
        lax.fori_loop(n * (quarter // 512), (n + 1) * (quarter // 512), reorder, 0)

    def make_tile(i, carry):
        pair = jnp.concatenate(
            [spread[pl.ds(2 * i, 64, stride=height), :], spread[pl.ds(2 * i + 1, 64, stride=height), :]], axis=0)
        tile = pair.T
        tiles[i + 1, 0] = tile[:64].astype(BF16)
        tiles[i + 1, 1] = tile[64:].astype(BF16)
        west_out[pl.ds(i, 1), :] = tile[:1]
        east_out[pl.ds(i, 1), :] = tile[127:]
        return carry

    lax.fori_loop(0, pairs, make_tile, 0, unroll=2)

    pl.semaphore_wait(barrier, greeted)
    copies = []

    def send(source, target, sem, which, landed):
        copy = pltpu.make_async_remote_copy(
            src_ref=source, dst_ref=target, send_sem=send_sem.at[sem], recv_sem=recv_sem.at[landed],
            device_id=beside(*which), device_id_type=MESH)
        copy.start()
        copies.append(copy)

    head, tail = pl.ds(0, 8), pl.ds(pairs - 8, 8)
    up_slot = jnp.where(at_north, 0, pairs + 1)
    down_slot = jnp.where(at_south, pairs + 1, 0)
    up_corner = pl.ds(pl.multiple_of(jnp.where(at_north, 0, pairs + 8), 8), 8)
    down_corner = pl.ds(pl.multiple_of(jnp.where(at_south, pairs + 8, 0), 8), 8)
    up_sem, down_sem = jnp.where(at_north, 0, 1), jnp.where(at_south, 1, 0)
    send(west_out, east_in.at[pl.ds(8, pairs)], 0, (lat, lon, -1), 6)
    send(east_out, west_in.at[pl.ds(8, pairs)], 1, (lat, lon, 1), 7)
    send(tiles.at[1, pl.ds(0, 2)], tiles.at[up_slot, pl.ds(0, 2)], 2, (up_lat, up_lon, 0), up_sem)
    send(tiles.at[pairs, pl.ds(0, 2)], tiles.at[down_slot, pl.ds(0, 2)], 3, (down_lat, down_lon, 0), down_sem)
    send(west_out.at[head], east_in.at[up_corner], 4, (up_lat, up_lon, -1), 2 + up_sem)
    send(east_out.at[head], west_in.at[up_corner], 5, (up_lat, up_lon, 1), 4 + up_sem)
    send(west_out.at[tail], east_in.at[down_corner], 6, (down_lat, down_lon, -1), 2 + down_sem)
    send(east_out.at[tail], west_in.at[down_corner], 7, (down_lat, down_lon, 1), 4 + down_sem)

    for load in loads[4:]:
        load.wait()

    def activate(n, carry):
        at = pl.ds(pl.multiple_of(n * 256, 256), 256)
        up = across(coarse_ref[at, :], tconv_ref[...])
        logistic = 0.5 * jnp.tanh(0.5 * up) + 0.5
        act_t[:, at] = (up * logistic).astype(BF16).T
        slope[at, :] = logistic * (1.0 + up * (1.0 - logistic))
        return carry

    lax.fori_loop(0, chunks, activate, 0)

    def block(tap):
        return conv_ref[:, 64 * tap : 64 * tap + 64]

    none = jnp.zeros((64, 64), BF16)
    places = {(s, w, h, p, q): t for s, w, h, p, q, t in window_blocks()}
    for s, w, h in [(s, w, h) for s in range(2) for w in range(4) for h in range(2)]:
        line = [block(places[s, w, h, p, q]) if (s, w, h, p, q) in places else none for p in range(2) for q in range(2)]
        at = w * 256 + s * 128 + h * 64
        weights[at : at + 64, :] = jnp.concatenate(line, axis=1)
    places = {(w, h, p, q): t for w, h, p, q, t in pole_blocks()}
    for w, h in [(w, h) for w in range(4) for h in range(2)]:
        line = [block(places[w, h, p, q]) if (w, h, p, q) in places else none for p in range(2) for q in range(2)]
        at = w * 128 + h * 64
        pole_weights[at : at + 64, :] = jnp.concatenate(line, axis=1)

    pole_extra[...] = jnp.zeros_like(pole_extra)
    pole_sums[...] = jnp.zeros_like(pole_sums)

    for landed, source in enumerate(
        (tiles.at[0, pl.ds(0, 2)], tiles.at[0, pl.ds(0, 2)], east_in.at[head], east_in.at[head], west_in.at[head],
         west_in.at[head], east_in.at[pl.ds(8, pairs)], west_in.at[pl.ds(8, pairs)])):
        pltpu.make_async_remote_copy(
            src_ref=source, dst_ref=source, send_sem=send_sem.at[0], recv_sem=recv_sem.at[landed],
            device_id=beside(lat, lon, 1), device_id_type=MESH).wait_recv()

    line = lax.broadcasted_iota(jnp.int32, (64, 128), 0)

    def shift(i, west_row, east_row):
        even, odd = tiles[i, 0].astype(F32), tiles[i, 1].astype(F32)
        tiles[i, 2] = jnp.where(line == 0, west_in[pl.ds(west_row, 1), :], pltpu.roll(odd, 1, 0)).astype(BF16)
        tiles[i, 3] = jnp.where(line == 63, east_in[pl.ds(east_row, 1), :], pltpu.roll(even, 63, 0)).astype(BF16)

    def shift_own(i, carry):
        shift(i, i + 7, i + 7)
        return carry

    north_row, south_row = jnp.where(at_north, 0, 7), jnp.where(at_south, pairs + 15, pairs + 8)
    shift(0, north_row, north_row)
    shift(pairs + 1, south_row, south_row)
    lax.fori_loop(1, pairs + 1, shift_own, 0, unroll=2)

    lane = lax.broadcasted_iota(jnp.int32, (64, 128), 1)
    blank = jnp.zeros((64, 128), BF16)

    def take_pole(slot, first, keep):
        for w in range(4):
            pole_patches[first : first + 64, 128 * w : 128 * w + 128] = jnp.where(keep, tiles[slot, w].astype(F32), 0.0).astype(BF16)
            pole_patches[64 - first : 128 - first, 128 * w : 128 * w + 128] = blank
            tiles[slot, w] = blank

    last = pairs * 64

    @pl.when(at_north)
    def _():
        take_pole(0, 0, lane < 64)
        pole_extra[0] = times(pole_patches[...], pole_weights[...])
        pole_sums[...] = times(act_t[:, :128], pole_patches[...])

    @pl.when(at_south)
    def _():
        take_pole(pairs + 1, 64, lane >= 64)
        pole_extra[1] = times(pole_patches[...], pole_weights[...])
        pole_sums[...] = times(act_t[:, last - 128 :], pole_patches[...])

    def lay(i, carry):
        at = pl.ds(pl.multiple_of(i * 64, 64), 64)
        for w in range(4):
            patches[at, 256 * w : 256 * w + 128] = tiles[i + 1, w]
            patches[at, 256 * w + 128 : 256 * w + 256] = jnp.where(lane < 64, tiles[i + 2, w], tiles[i, w])
        return carry

    lax.fori_loop(0, pairs, lay, 0, unroll=2)

    for n in range(chunks):
        at = slice(n * 256, n * 256 + 256)
        grad = times(patches[at, :], weights[...])
        if n == 0:
            grad = jnp.concatenate([grad[:128] + pole_extra[0], grad[128:]], axis=0)
        if n == chunks - 1:
            grad = jnp.concatenate([grad[:128], grad[128:] + pole_extra[1]], axis=0)
        rounded = (grad * slope[at, :]).astype(BF16)
        pre[at, :] = rounded
        pre_t[:, at] = rounded.T
    members = shares.shape[1]
    share = 256 // members
    spare = 16 // members
    taps_grad = times(pre_t[...], coarse_ref[...])
    for m in range(members):
        shares[1, m, :share] = taps_grad[share * m : share * m + share]

    found = {}

    def add(tap, value):
        found[tap] = value if tap not in found else found[tap] + value

    for w in range(4):
        grads = times(act_t[...], patches[:, 256 * w : 256 * w + 256])
        for s, ww, h, p, q, t in window_blocks():
            if ww == w:
                at, col = 128 * p + 64 * q, s * 128 + h * 64
                add(t, grads[at : at + 64, col : col + 64])
    for w, h, p, q, t in pole_blocks():
        at, col = 128 * p + 64 * q, w * 128 + h * 64
        add(t, pole_sums[at : at + 64, col : col + 64])
    for b in range(4):
        both = jnp.concatenate([found[2 * b], found[2 * b + 1]], axis=0).T
        for m in range(members):
            low, high = max(64 * b, share * m), min(64 * b + 64, share * m + share)
            if low < high:
                shares[0, m, low - share * m : high - share * m] = both[low - 64 * b : high - 64 * b]
    last_tap = found[8].T
    last_tap = jnp.concatenate([last_tap[:32], last_tap[32:]], axis=1)
    for m in range(members):
        for core in range(2):
            at = 16 * core + spare * m
            shares[core, m, share:] = last_tap[at : at + spare]
    total.start()

    for n in range(chunks):
        at = slice(n * 256, n * 256 + 256)
        out_ref[at, :] = times(pre[at, :], tconv_ref[...]).astype(BF16)
    total.scatter()
    total.pass_on()
    total.give_back()
    total.bring_home()
    for copy in copies:
        copy.wait_send()
    total.end()
    for m in range(members):
        taps_out[share * m : share * m + share, :] = final[1, m, :share]
        for low in range(share * m, share * m + share, min(share, 64)):
            high, b = low + min(share, 64), low // 64
            conv_out[low - 64 * b : high - 64 * b, 128 * b : 128 * b + 128] = final[0, m, low - share * m : high - share * m]
        for core in range(2):
            at = 16 * core + spare * m
            line = final[core, m, share:]
            conv_out[at : at + spare, 512:] = line[:, :64]
            conv_out[32 + at : 32 + at + spare, 512:] = line[:, 64:]


def section(scale, coarse, cotangent, tconv, conv):
    cells = coarse.shape[0]
    pairs = cells // 64
    members, length = 2 * lax.axis_size("lat"), lax.axis_size("lon") // 4
    chunk = 272 // members
    vmem, hbm = pl.BlockSpec(memory_space=pltpu.VMEM), pl.BlockSpec(memory_space=pltpu.HBM)
    return pl.pallas_call(
        functools.partial(section_kernel, scale),
        out_shape=(jax.ShapeDtypeStruct((cells, 128), BF16), jax.ShapeDtypeStruct((256, 128), F32),
                   jax.ShapeDtypeStruct(conv.shape, F32)),
        in_specs=[hbm] * 4,
        out_specs=(vmem, vmem, vmem),
        scratch_shapes=[
            pltpu.VMEM(coarse.shape, BF16), pltpu.VMEM(cotangent.shape, BF16), pltpu.VMEM(tconv.shape, BF16),
            pltpu.VMEM(conv.shape, BF16),
            pltpu.VMEM((cells * 2, 128), F32),
            pltpu.VMEM((pairs + 2, 4, 64, 128), BF16),
            pltpu.VMEM((pairs, 128), F32), pltpu.VMEM((pairs, 128), F32),
            pltpu.VMEM((pairs + 16, 128), F32), pltpu.VMEM((pairs + 16, 128), F32),
            pltpu.VMEM((cells, 1024), BF16),
            pltpu.VMEM((256, cells), BF16),
            pltpu.VMEM((cells, 256), F32),
            pltpu.VMEM((cells, 256), BF16),
            pltpu.VMEM((256, cells), BF16),
            pltpu.VMEM((1024, 256), BF16),
            pltpu.VMEM((512, 256), BF16),
            pltpu.VMEM((128, 512), BF16),
            pltpu.VMEM((2, 128, 256), F32),
            pltpu.VMEM((256, 512), F32),
            pltpu.SemaphoreType.DMA((8,)), pltpu.SemaphoreType.DMA((8,)), pltpu.SemaphoreType.DMA((7,)),
            pltpu.VMEM((2, members, chunk, 128), F32),
            pltpu.VMEM((members, chunk, 128), F32), pltpu.VMEM((members, chunk, 128), F32),
            pltpu.VMEM((members, chunk, 128), F32), pltpu.VMEM((length, chunk, 128), F32),
            pltpu.VMEM((2, members, chunk, 128), F32),
            pltpu.SemaphoreType.DMA((5,)), pltpu.SemaphoreType.DMA((5,)),
        ],
        compiler_params=pltpu.CompilerParams(collective_id=0, has_side_effects=True, vmem_limit_bytes=VMEM_LIMIT),
        name="section",
    )(coarse, cotangent, tconv, conv)


def per_device(coarse_field, cotangent, tconv_weight, conv_weight):
    batch, channels, rows_here, cols_here = cotangent.shape
    in_channels = coarse_field.shape[1]
    coarse = coarse_field.transpose(0, 2, 3, 1).reshape(-1, in_channels)
    total_cells = batch * rows_here * cols_here * lax.axis_size("lat") * lax.axis_size("lon")
    coarse_grad, tconv_grad, conv_grad = section(
        1.0 / math.sqrt(total_cells), coarse, cotangent.reshape(channels * rows_here, cols_here),
        tconv_weight.reshape(4 * channels, in_channels), conv_weight)
    coarse_grad = coarse_grad.reshape(batch, rows_here // 2, cols_here // 2, in_channels).transpose(0, 3, 1, 2)
    return coarse_grad, tconv_grad.reshape(4, channels, in_channels), conv_grad


def solution(mesh):
    return jax.shard_map(
        per_device,
        mesh=mesh,
        in_specs=(P(None, None, "lat", "lon"), P(None, None, "lat", "lon"), P(), P()),
        out_specs=(P(None, None, "lat", "lon"), P(), P()),
        check_vma=False,
    )
```

```python
import functools
import math

import jax
import jax.numpy as jnp
from jax import lax
from jax.experimental import pallas as pl
from jax.experimental.pallas import tpu as pltpu
from jax.sharding import PartitionSpec as P

MESH = pl.DeviceIdType.MESH
F32, BF16 = jnp.float32, jnp.bfloat16
OWN, BESIDE = 0, 1
VMEM_LIMIT = 48 * 2**20


def row_step(source, half, p):
    step = p - half if source == OWN else (p - 2 if half == 0 else p + 1)
    return step if abs(step) <= 1 else None


def col_step(window, q):
    step = (q, q - 1, q + 1, q - 2)[window]
    return step if abs(step) <= 1 else None


def window_blocks():
    for source in (OWN, BESIDE):
        for window in range(4):
            for half in range(2):
                for p in range(2):
                    for q in range(2):
                        a, b = row_step(source, half, p), col_step(window, q)
                        if a is not None and b is not None:
                            yield source, window, half, p, q, 3 * (a + 1) + b + 1


def pole_blocks():
    for window in range(4):
        for half in range(2):
            for q in range(2):
                b = col_step(window, q)
                if b is not None:
                    yield window, half, half, q, 3 * (2 * half) + b + 1


def across(a, b):
    return lax.dot_general(a, b, (((1,), (1,)), ((), ())), preferred_element_type=F32)


def times(a, b):
    return jnp.dot(a, b, preferred_element_type=F32)


def each(low, high, act):
    def step(n, carry):
        act(n)
        return carry

    lax.fori_loop(low, high, step, 0)


class Sum:
    def __init__(self, source, half, arrived, seen, along, final, scale, send, recv):
        self.source, self.half, self.arrived, self.seen, self.along, self.final = source, half, arrived, seen, along, final
        self.scale, self.send, self.recv = scale, send, recv
        self.lat, lon = lax.axis_index("lat"), lax.axis_index("lon")
        self.lats, lons = lax.axis_size("lat"), lax.axis_size("lon")
        self.side = lons // 2
        self.members, self.length = 2 * self.lats, lons // 4
        self.far = jnp.where(lon >= self.side, 1, 0)
        self.near = lon - self.far * self.side
        self.z, self.core = self.near // 2, self.near % 2
        self.mine = self.far * self.lats + self.lat

    def other(self):
        return {"lat": self.lat, "lon": self.far * self.side + self.z * 2 + 1 - self.core}

    def member(self, d):
        flip = d >= self.lats
        lat = self.lat + jnp.where(flip, d - self.lats, d)
        return jnp.where(lat >= self.lats, lat - self.lats, lat), jnp.where(flip, 1 - self.far, self.far)

    def plane(self, d):
        lat, far = self.member(d)
        return {"lat": lat, "lon": far * self.side + self.near}

    def line(self, e):
        z = self.z + e
        z = jnp.where(z >= self.length, z - self.length, z)
        return {"lat": self.lat, "lon": self.far * self.side + z * 2 + self.core}

    def copy(self, source, target, phase, where):
        return pltpu.make_async_remote_copy(
            src_ref=source, dst_ref=target, send_sem=self.send.at[phase], recv_sem=self.recv.at[phase], device_id=where,
            device_id_type=MESH)

    def greet(self, barrier):
        def signal(peer):
            pl.semaphore_signal(barrier, inc=1, device_id=peer, device_id_type=MESH)

        signal(self.other())
        each(1, self.members, lambda d: signal(self.plane(d)))
        each(1, self.length, lambda e: signal(self.line(e)))
        return self.members + self.length - 1

    def all_of(self, phase):
        part = (self.arrived, self.seen.at[pl.ds(1, self.members - 1)], self.along.at[pl.ds(1, self.length - 1)],
                self.seen.at[pl.ds(1, self.members - 1)], self.arrived)[phase]
        return self.copy(part, part, phase, self.other())

    def start(self):
        self.copy(self.source.at[1 - self.core], self.arrived, 0, self.other()).start()

    def scatter(self):
        self.all_of(0).wait_recv()
        self.half[...] = self.source[self.core] + self.arrived[...]

        def send(d):
            lat, far = self.member(d)
            self.copy(self.half.at[far * self.lats + lat], self.seen.at[d], 1, self.plane(d)).start()

        each(1, self.members, send)

    def pass_on(self):
        self.all_of(1).wait_recv()
        total = self.half[self.mine]
        for d in range(1, self.members):
            total = total + self.seen[d]
        self.along[self.z] = total
        each(1, self.length, lambda e: self.copy(self.along.at[self.z], self.along.at[self.z], 2, self.line(e)).start())

    def give_back(self):
        self.all_of(2).wait_recv()
        total = self.along[0]
        for z in range(1, self.length):
            total = total + self.along[z]
        self.final[self.core, self.mine] = total * self.scale
        at = self.final.at[self.core, self.mine]
        each(1, self.members, lambda d: self.copy(at, at, 3, self.plane(d)).start())

    def bring_home(self):
        self.all_of(3).wait_recv()
        self.copy(self.final.at[self.core], self.final.at[self.core], 4, self.other()).start()

    def end(self):
        self.all_of(4).wait_recv()
        for phase in range(5):
            self.all_of(phase).wait_send()


def section_kernel(
    scale, coarse_hbm, cot_hbm, tconv_hbm, conv_hbm, out_ref, taps_out, conv_out,
    coarse_ref, cot_ref, tconv_ref, conv_ref,
    spread, tiles, west_out, east_out, west_in, east_in, patches, act_t, slope, pre, pre_t, weights, pole_weights,
    pole_patches, pole_extra, pole_sums, send_sem, recv_sem, load_sem,
    shares, half, arrived, seen, along, final, sum_send, sum_recv,
):
    pairs = coarse_ref.shape[0] // 64
    chunks = pairs // 4
    loads = []
    quarter = cot_ref.shape[0] // 4
    for n in range(4):
        at = pl.ds(n * quarter, quarter)
        loads.append(pltpu.make_async_copy(cot_hbm.at[at], cot_ref.at[at], load_sem.at[n]))
    for n, (source, target) in enumerate(((coarse_hbm, coarse_ref), (tconv_hbm, tconv_ref), (conv_hbm, conv_ref))):
        loads.append(pltpu.make_async_copy(source, target, load_sem.at[4 + n]))
    for load in loads:
        load.start()

    lat, lon = lax.axis_index("lat"), lax.axis_index("lon")
    lats, lons = lax.axis_size("lat"), lax.axis_size("lon")
    at_north, at_south = lat == 0, lat == lats - 1
    opposite = lax.rem(lon + lons // 2, lons)
    up_lat, up_lon = jnp.where(at_north, 0, lat - 1), jnp.where(at_north, opposite, lon)
    down_lat, down_lon = jnp.where(at_south, lats - 1, lat + 1), jnp.where(at_south, opposite, lon)

    def beside(which_lat, which_lon, by):
        return {"lat": which_lat, "lon": lax.rem(which_lon + by + lons, lons)}

    total = Sum(shares, half, arrived, seen, along, final, scale, sum_send, sum_recv)

    barrier = pltpu.get_barrier_semaphore()
    greeted = 8 + total.greet(barrier)
    for which in ((lat, lon, -1), (lat, lon, 1), (up_lat, up_lon, -1), (up_lat, up_lon, 0), (up_lat, up_lon, 1),
                  (down_lat, down_lon, -1), (down_lat, down_lon, 0), (down_lat, down_lon, 1)):
        pl.semaphore_signal(barrier, inc=1, device_id=beside(*which), device_id_type=MESH)

    rows, cols = lax.broadcasted_iota(jnp.int32, (128, 128), 0), lax.broadcasted_iota(jnp.int32, (128, 128), 1)
    order = jnp.where(rows == (cols % 64) * 2 + cols // 64, 1.0, 0.0).astype(BF16)
    height = 2 * pairs

    def reorder(n, carry):
        at = pl.ds(pl.multiple_of(n * 512, 512), 512)
        spread[at, :] = times(cot_ref[at, :], order)
        return carry

    for n in range(4):
        loads[n].wait()
        lax.fori_loop(n * (quarter // 512), (n + 1) * (quarter // 512), reorder, 0)

    def make_tile(i, carry):
        pair = jnp.concatenate(
            [spread[pl.ds(2 * i, 64, stride=height), :], spread[pl.ds(2 * i + 1, 64, stride=height), :]], axis=0)
        tile = pair.T
        tiles[i + 1, 0] = tile[:64].astype(BF16)
        tiles[i + 1, 1] = tile[64:].astype(BF16)
        west_out[pl.ds(i, 1), :] = tile[:1]
        east_out[pl.ds(i, 1), :] = tile[127:]
        return carry

    lax.fori_loop(0, pairs, make_tile, 0, unroll=2)

    pl.semaphore_wait(barrier, greeted)
    copies = []

    def send(source, target, sem, which, landed):
        copy = pltpu.make_async_remote_copy(
            src_ref=source, dst_ref=target, send_sem=send_sem.at[sem], recv_sem=recv_sem.at[landed],
            device_id=beside(*which), device_id_type=MESH)
        copy.start()
        copies.append(copy)

    head, tail = pl.ds(0, 8), pl.ds(pairs - 8, 8)
    up_slot = jnp.where(at_north, 0, pairs + 1)
    down_slot = jnp.where(at_south, pairs + 1, 0)
    up_corner = pl.ds(pl.multiple_of(jnp.where(at_north, 0, pairs + 8), 8), 8)
    down_corner = pl.ds(pl.multiple_of(jnp.where(at_south, pairs + 8, 0), 8), 8)
    up_sem, down_sem = jnp.where(at_north, 0, 1), jnp.where(at_south, 1, 0)
    send(west_out, east_in.at[pl.ds(8, pairs)], 0, (lat, lon, -1), 6)
    send(east_out, west_in.at[pl.ds(8, pairs)], 1, (lat, lon, 1), 7)
    send(tiles.at[1], tiles.at[up_slot], 2, (up_lat, up_lon, 0), up_sem)
    send(tiles.at[pairs], tiles.at[down_slot], 3, (down_lat, down_lon, 0), down_sem)
    send(west_out.at[head], east_in.at[up_corner], 4, (up_lat, up_lon, -1), 2 + up_sem)
    send(east_out.at[head], west_in.at[up_corner], 5, (up_lat, up_lon, 1), 4 + up_sem)
    send(west_out.at[tail], east_in.at[down_corner], 6, (down_lat, down_lon, -1), 2 + down_sem)
    send(east_out.at[tail], west_in.at[down_corner], 7, (down_lat, down_lon, 1), 4 + down_sem)

    row = lax.broadcasted_iota(jnp.int32, (64, 128), 0)

    def beside_tile(even, odd, west_row, east_row):
        return (jnp.where(row == 0, west_row, pltpu.roll(odd, 1, 0)), jnp.where(row == 63, east_row, pltpu.roll(even, 63, 0)))

    def place(i, w, low, high, value):
        def at(block):
            return pl.ds(pl.multiple_of(block * 64 + low, 16), high - low)

        patches[at(i + 1), 256 * w : 256 * w + 128] = value
        patches[at(i), 256 * w + 128 : 256 * w + 192] = value[:, :64]
        patches[at(i + 2), 256 * w + 192 : 256 * w + 256] = value[:, 64:]

    def lay(i, carry):
        even, odd = tiles[i + 1, 0], tiles[i + 1, 1]
        west, east = beside_tile(even.astype(F32), odd.astype(F32), 0.0, 0.0)
        for w, value in enumerate((even, odd, west.astype(BF16), east.astype(BF16))):
            place(i, w, 0, 64, value)
        return carry

    lax.fori_loop(0, pairs, lay, 0, unroll=2)

    for load in loads[4:]:
        load.wait()

    def activate(n, carry):
        at = pl.ds(pl.multiple_of(n * 256, 256), 256)
        up = across(coarse_ref[at, :], tconv_ref[...])
        logistic = 0.5 * jnp.tanh(0.5 * up) + 0.5
        act_t[:, at] = (up * logistic).astype(BF16).T
        slope[at, :] = logistic * (1.0 + up * (1.0 - logistic))
        return carry

    lax.fori_loop(0, chunks, activate, 0)

    def block(tap):
        return conv_ref[:, 64 * tap : 64 * tap + 64]

    none = jnp.zeros((64, 64), BF16)
    places = {(s, w, h, p, q): t for s, w, h, p, q, t in window_blocks()}
    for s, w, h in [(s, w, h) for s in range(2) for w in range(4) for h in range(2)]:
        line = [block(places[s, w, h, p, q]) if (s, w, h, p, q) in places else none for p in range(2) for q in range(2)]
        at = w * 256 + s * 128 + h * 64
        weights[at : at + 64, :] = jnp.concatenate(line, axis=1)
    places = {(w, h, p, q): t for w, h, p, q, t in pole_blocks()}
    for w, h in [(w, h) for w in range(4) for h in range(2)]:
        line = [block(places[w, h, p, q]) if (w, h, p, q) in places else none for p in range(2) for q in range(2)]
        at = w * 128 + h * 64
        pole_weights[at : at + 64, :] = jnp.concatenate(line, axis=1)

    pole_extra[...] = jnp.zeros_like(pole_extra)
    pole_sums[...] = jnp.zeros_like(pole_sums)

    for landed, source in enumerate(
        (tiles.at[0], tiles.at[0], east_in.at[head], east_in.at[head], west_in.at[head],
         west_in.at[head], east_in.at[pl.ds(8, pairs)], west_in.at[pl.ds(8, pairs)])):
        pltpu.make_async_remote_copy(
            src_ref=source, dst_ref=source, send_sem=send_sem.at[0], recv_sem=recv_sem.at[landed],
            device_id=beside(lat, lon, 1), device_id_type=MESH).wait_recv()

    edge = lax.broadcasted_iota(jnp.int32, (16, 128), 0)

    def mend(i, carry):
        for w, low, at_row, halo in ((2, 0, 0, west_in), (3, 48, 15, east_in)):
            block = patches[pl.ds(pl.multiple_of((i + 1) * 64 + low, 16), 16), 256 * w : 256 * w + 128].astype(F32)
            block = jnp.where(edge == at_row, halo[pl.ds(i + 8, 1), :], block).astype(BF16)
            place(i, w, low, low + 16, block)
        return carry

    lax.fori_loop(0, pairs, mend, 0, unroll=2)

    def halo_windows(slot, corner):
        even, odd = tiles[slot, 0].astype(F32), tiles[slot, 1].astype(F32)
        return (even, odd) + beside_tile(even, odd, west_in[pl.ds(corner, 1), :], east_in[pl.ds(corner, 1), :])

    north = halo_windows(0, jnp.where(at_north, 0, 7))
    south = halo_windows(pairs + 1, jnp.where(at_south, pairs + 15, pairs + 8))
    last = pairs * 64
    for w in range(4):
        patches[64:128, 256 * w + 192 : 256 * w + 256] = jnp.where(at_north, 0.0, north[w][:, 64:]).astype(BF16)
        patches[last : last + 64, 256 * w + 128 : 256 * w + 192] = jnp.where(at_south, 0.0, south[w][:, :64]).astype(BF16)

    lane = lax.broadcasted_iota(jnp.int32, (64, 128), 1)
    blank = jnp.zeros((64, 128), BF16)

    @pl.when(at_north)
    def _():
        for w in range(4):
            pole_patches[:64, 128 * w : 128 * w + 128] = jnp.where(lane < 64, north[w], 0.0).astype(BF16)
            pole_patches[64:, 128 * w : 128 * w + 128] = blank
        pole_extra[0] = times(pole_patches[...], pole_weights[...])
        pole_sums[...] = times(act_t[:, :128], pole_patches[...])

    @pl.when(at_south)
    def _():
        for w in range(4):
            pole_patches[:64, 128 * w : 128 * w + 128] = blank
            pole_patches[64:, 128 * w : 128 * w + 128] = jnp.where(lane < 64, 0.0, south[w]).astype(BF16)
        pole_extra[1] = times(pole_patches[...], pole_weights[...])
        pole_sums[...] = times(act_t[:, last - 128 :], pole_patches[...])

    for n in range(chunks):
        at = slice(n * 256, n * 256 + 256)
        grad = times(patches[n * 256 + 64 : n * 256 + 320, :], weights[...])
        if n == 0:
            grad = jnp.concatenate([grad[:128] + pole_extra[0], grad[128:]], axis=0)
        if n == chunks - 1:
            grad = jnp.concatenate([grad[:128], grad[128:] + pole_extra[1]], axis=0)
        rounded = (grad * slope[at, :]).astype(BF16)
        pre[at, :] = rounded
        pre_t[:, at] = rounded.T
    members = shares.shape[1]
    share = 256 // members
    spare = 16 // members
    taps_grad = times(pre_t[...], coarse_ref[...])
    for m in range(members):
        shares[1, m, :share] = taps_grad[share * m : share * m + share]

    found = {}

    def add(tap, value):
        found[tap] = value if tap not in found else found[tap] + value

    for w in range(4):
        grads = times(act_t[...], patches[64 : last + 64, 256 * w : 256 * w + 256])
        for s, ww, h, p, q, t in window_blocks():
            if ww == w:
                at, col = 128 * p + 64 * q, s * 128 + h * 64
                add(t, grads[at : at + 64, col : col + 64])
    for w, h, p, q, t in pole_blocks():
        at, col = 128 * p + 64 * q, w * 128 + h * 64
        add(t, pole_sums[at : at + 64, col : col + 64])
    for b in range(4):
        both = jnp.concatenate([found[2 * b], found[2 * b + 1]], axis=0).T
        for m in range(members):
            low, high = max(64 * b, share * m), min(64 * b + 64, share * m + share)
            if low < high:
                shares[0, m, low - share * m : high - share * m] = both[low - 64 * b : high - 64 * b]
    last_tap = found[8].T
    last_tap = jnp.concatenate([last_tap[:32], last_tap[32:]], axis=1)
    for m in range(members):
        for core in range(2):
            at = 16 * core + spare * m
            shares[core, m, share:] = last_tap[at : at + spare]
    total.start()

    for n in range(chunks):
        at = slice(n * 256, n * 256 + 256)
        out_ref[at, :] = times(pre[at, :], tconv_ref[...]).astype(BF16)
    total.scatter()
    total.pass_on()
    total.give_back()
    total.bring_home()
    for copy in copies:
        copy.wait_send()
    total.end()
    for m in range(members):
        taps_out[share * m : share * m + share, :] = final[1, m, :share]
        for low in range(share * m, share * m + share, min(share, 64)):
            high, b = low + min(share, 64), low // 64
            conv_out[low - 64 * b : high - 64 * b, 128 * b : 128 * b + 128] = final[0, m, low - share * m : high - share * m]
        for core in range(2):
            at = 16 * core + spare * m
            line = final[core, m, share:]
            conv_out[at : at + spare, 512:] = line[:, :64]
            conv_out[32 + at : 32 + at + spare, 512:] = line[:, 64:]


def section(scale, coarse, cotangent, tconv, conv):
    cells = coarse.shape[0]
    pairs = cells // 64
    members, length = 2 * lax.axis_size("lat"), lax.axis_size("lon") // 4
    chunk = 272 // members
    vmem, hbm = pl.BlockSpec(memory_space=pltpu.VMEM), pl.BlockSpec(memory_space=pltpu.HBM)
    return pl.pallas_call(
        functools.partial(section_kernel, scale),
        out_shape=(pltpu.VMEM((cells, 128), BF16), pltpu.VMEM((256, 128), F32), pltpu.VMEM(conv.shape, F32)),
        in_specs=[hbm] * 4,
        out_specs=(vmem, vmem, vmem),
        scratch_shapes=[
            pltpu.VMEM(coarse.shape, BF16), pltpu.VMEM(cotangent.shape, BF16), pltpu.VMEM(tconv.shape, BF16),
            pltpu.VMEM(conv.shape, BF16),
            pltpu.VMEM((cells * 2, 128), F32),
            pltpu.VMEM((pairs + 2, 2, 64, 128), BF16),
            pltpu.VMEM((pairs, 128), F32), pltpu.VMEM((pairs, 128), F32),
            pltpu.VMEM((pairs + 16, 128), F32), pltpu.VMEM((pairs + 16, 128), F32),
            pltpu.VMEM((cells + 128, 1024), BF16),
            pltpu.VMEM((256, cells), BF16),
            pltpu.VMEM((cells, 256), F32),
            pltpu.VMEM((cells, 256), BF16),
            pltpu.VMEM((256, cells), BF16),
            pltpu.VMEM((1024, 256), BF16),
            pltpu.VMEM((512, 256), BF16),
            pltpu.VMEM((128, 512), BF16),
            pltpu.VMEM((2, 128, 256), F32),
            pltpu.VMEM((256, 512), F32),
            pltpu.SemaphoreType.DMA((8,)), pltpu.SemaphoreType.DMA((8,)), pltpu.SemaphoreType.DMA((7,)),
            pltpu.VMEM((2, members, chunk, 128), F32),
            pltpu.VMEM((members, chunk, 128), F32), pltpu.VMEM((members, chunk, 128), F32),
            pltpu.VMEM((members, chunk, 128), F32), pltpu.VMEM((length, chunk, 128), F32),
            pltpu.VMEM((2, members, chunk, 128), F32),
            pltpu.SemaphoreType.DMA((5,)), pltpu.SemaphoreType.DMA((5,)),
        ],
        compiler_params=pltpu.CompilerParams(collective_id=0, has_side_effects=True, vmem_limit_bytes=VMEM_LIMIT),
        name="section",
    )(*(pltpu.with_memory_space_constraint(x, pltpu.HBM) for x in (coarse, cotangent, tconv, conv)))


def per_device(coarse_field, cotangent, tconv_weight, conv_weight):
    batch, channels, rows_here, cols_here = cotangent.shape
    in_channels = coarse_field.shape[1]
    coarse = coarse_field.transpose(0, 2, 3, 1).reshape(-1, in_channels)
    total_cells = batch * rows_here * cols_here * lax.axis_size("lat") * lax.axis_size("lon")
    coarse_grad, tconv_grad, conv_grad = section(
        1.0 / math.sqrt(total_cells), coarse, cotangent.reshape(channels * rows_here, cols_here),
        tconv_weight.reshape(4 * channels, in_channels), conv_weight)
    coarse_grad = coarse_grad.reshape(batch, rows_here // 2, cols_here // 2, in_channels).transpose(0, 3, 1, 2)
    return coarse_grad, tconv_grad.reshape(4, channels, in_channels), conv_grad


def solution(mesh):
    return jax.shard_map(
        per_device,
        mesh=mesh,
        in_specs=(P(None, None, "lat", "lon"), P(None, None, "lat", "lon"), P(), P()),
        out_specs=(P(None, None, "lat", "lon"), P(), P()),
        check_vma=False,
    )
```

```python
import functools
import math

import jax
import jax.numpy as jnp
from jax import lax
from jax.experimental import pallas as pl
from jax.experimental.pallas import tpu as pltpu
from jax.sharding import PartitionSpec as P

MESH = pl.DeviceIdType.MESH
F32, BF16 = jnp.float32, jnp.bfloat16
OWN, BESIDE = 0, 1
VMEM_LIMIT = 48 * 2**20


def row_step(source, half, p):
    step = p - half if source == OWN else (p - 2 if half == 0 else p + 1)
    return step if abs(step) <= 1 else None


def col_step(window, q):
    step = (q, q - 1, q + 1, q - 2)[window]
    return step if abs(step) <= 1 else None


def window_blocks():
    for source in (OWN, BESIDE):
        for window in range(4):
            for half in range(2):
                for p in range(2):
                    for q in range(2):
                        a, b = row_step(source, half, p), col_step(window, q)
                        if a is not None and b is not None:
                            yield source, window, half, p, q, 3 * (a + 1) + b + 1


def pole_blocks():
    for window in range(4):
        for half in range(2):
            for q in range(2):
                b = col_step(window, q)
                if b is not None:
                    yield window, half, half, q, 3 * (2 * half) + b + 1


def across(a, b):
    return lax.dot_general(a, b, (((1,), (1,)), ((), ())), preferred_element_type=F32)


def times(a, b):
    return jnp.dot(a, b, preferred_element_type=F32)


def each(low, high, act):
    def step(n, carry):
        act(n)
        return carry

    lax.fori_loop(low, high, step, 0)


class Sum:
    def __init__(self, source, half, arrived, seen, along, final, scale, send, recv):
        self.source, self.half, self.arrived, self.seen, self.along, self.final = source, half, arrived, seen, along, final
        self.scale, self.send, self.recv = scale, send, recv
        self.lat, lon = lax.axis_index("lat"), lax.axis_index("lon")
        self.lats, lons = lax.axis_size("lat"), lax.axis_size("lon")
        self.side = lons // 2
        self.members, self.length = 2 * self.lats, lons // 4
        self.far = jnp.where(lon >= self.side, 1, 0)
        self.near = lon - self.far * self.side
        self.z, self.core = self.near // 2, self.near % 2
        self.mine = self.far * self.lats + self.lat

    def other(self):
        return {"lat": self.lat, "lon": self.far * self.side + self.z * 2 + 1 - self.core}

    def member(self, d):
        flip = d >= self.lats
        lat = self.lat + jnp.where(flip, d - self.lats, d)
        return jnp.where(lat >= self.lats, lat - self.lats, lat), jnp.where(flip, 1 - self.far, self.far)

    def plane(self, d):
        lat, far = self.member(d)
        return {"lat": lat, "lon": far * self.side + self.near}

    def line(self, e):
        z = self.z + e
        z = jnp.where(z >= self.length, z - self.length, z)
        return {"lat": self.lat, "lon": self.far * self.side + z * 2 + self.core}

    def copy(self, source, target, phase, where):
        return pltpu.make_async_remote_copy(
            src_ref=source, dst_ref=target, send_sem=self.send.at[phase], recv_sem=self.recv.at[phase], device_id=where,
            device_id_type=MESH)

    def greet(self, barrier):
        def signal(peer):
            pl.semaphore_signal(barrier, inc=1, device_id=peer, device_id_type=MESH)

        signal(self.other())
        each(1, self.members, lambda d: signal(self.plane(d)))
        each(1, self.length, lambda e: signal(self.line(e)))
        return self.members + self.length - 1

    def all_of(self, phase):
        part = (self.arrived, self.seen.at[pl.ds(1, self.members - 1)], self.along.at[pl.ds(1, self.length - 1)],
                self.seen.at[pl.ds(1, self.members - 1)], self.arrived)[phase]
        return self.copy(part, part, phase, self.other())

    def start(self):
        self.copy(self.source.at[1 - self.core], self.arrived, 0, self.other()).start()

    def scatter(self):
        self.all_of(0).wait_recv()
        self.half[...] = self.source[self.core] + self.arrived[...]

        def send(d):
            lat, far = self.member(d)
            self.copy(self.half.at[far * self.lats + lat], self.seen.at[d], 1, self.plane(d)).start()

        each(1, self.members, send)

    def pass_on(self):
        self.all_of(1).wait_recv()
        total = self.half[self.mine]
        for d in range(1, self.members):
            total = total + self.seen[d]
        self.along[self.z] = total
        each(1, self.length, lambda e: self.copy(self.along.at[self.z], self.along.at[self.z], 2, self.line(e)).start())

    def give_back(self):
        self.all_of(2).wait_recv()
        total = self.along[0]
        for z in range(1, self.length):
            total = total + self.along[z]
        self.final[self.core, self.mine] = total * self.scale
        at = self.final.at[self.core, self.mine]
        each(1, self.members, lambda d: self.copy(at, at, 3, self.plane(d)).start())

    def bring_home(self):
        self.all_of(3).wait_recv()
        self.copy(self.final.at[self.core], self.final.at[self.core], 4, self.other()).start()

    def end(self):
        self.all_of(4).wait_recv()
        for phase in range(5):
            self.all_of(phase).wait_send()


def section_kernel(
    scale, coarse_hbm, cot_hbm, tconv_hbm, conv_hbm, out_ref, taps_out, conv_out,
    coarse_ref, cot_ref, tconv_ref, conv_ref,
    spread, tiles, west_out, east_out, west_in, east_in, patches, act_t, slope, pre, pre_t, weights, pole_weights,
    pole_patches, pole_extra, pole_sums, send_sem, recv_sem, load_sem,
    shares, half, arrived, seen, along, final, sum_send, sum_recv,
):
    pairs = coarse_ref.shape[0] // 64
    chunks = pairs // 4
    loads = []
    quarter = cot_ref.shape[0] // 4
    for n in range(4):
        at = pl.ds(n * quarter, quarter)
        loads.append(pltpu.make_async_copy(cot_hbm.at[at], cot_ref.at[at], load_sem.at[n]))
    for n, (source, target) in enumerate(((coarse_hbm, coarse_ref), (tconv_hbm, tconv_ref), (conv_hbm, conv_ref))):
        loads.append(pltpu.make_async_copy(source, target, load_sem.at[4 + n]))
    for load in loads:
        load.start()

    lat, lon = lax.axis_index("lat"), lax.axis_index("lon")
    lats, lons = lax.axis_size("lat"), lax.axis_size("lon")
    at_north, at_south = lat == 0, lat == lats - 1
    opposite = lax.rem(lon + lons // 2, lons)
    up_lat, up_lon = jnp.where(at_north, 0, lat - 1), jnp.where(at_north, opposite, lon)
    down_lat, down_lon = jnp.where(at_south, lats - 1, lat + 1), jnp.where(at_south, opposite, lon)

    def beside(which_lat, which_lon, by):
        return {"lat": which_lat, "lon": lax.rem(which_lon + by + lons, lons)}

    total = Sum(shares, half, arrived, seen, along, final, scale, sum_send, sum_recv)

    barrier = pltpu.get_barrier_semaphore()
    greeted = 8 + total.greet(barrier)
    for which in ((lat, lon, -1), (lat, lon, 1), (up_lat, up_lon, -1), (up_lat, up_lon, 0), (up_lat, up_lon, 1),
                  (down_lat, down_lon, -1), (down_lat, down_lon, 0), (down_lat, down_lon, 1)):
        pl.semaphore_signal(barrier, inc=1, device_id=beside(*which), device_id_type=MESH)

    rows, cols = lax.broadcasted_iota(jnp.int32, (128, 128), 0), lax.broadcasted_iota(jnp.int32, (128, 128), 1)
    order = jnp.where(rows == (cols % 64) * 2 + cols // 64, 1.0, 0.0).astype(BF16)
    height = 2 * pairs

    def reorder(n, carry):
        at = pl.ds(pl.multiple_of(n * 512, 512), 512)
        spread[at, :] = times(cot_ref[at, :], order)
        return carry

    for n in range(4):
        loads[n].wait()
        lax.fori_loop(n * (quarter // 512), (n + 1) * (quarter // 512), reorder, 0, unroll=True)

    def make_tile(i, carry):
        pair = jnp.concatenate(
            [spread[pl.ds(2 * i, 64, stride=height), :], spread[pl.ds(2 * i + 1, 64, stride=height), :]], axis=0)
        tile = pair.astype(BF16).T
        tiles[i + 1, 0] = tile[:64]
        tiles[i + 1, 1] = tile[64:]
        west_out[pl.ds(i, 1), :] = tile[:16].astype(F32)[:1]
        east_out[pl.ds(i, 1), :] = tile[112:].astype(F32)[15:]
        return carry

    lax.fori_loop(0, pairs, make_tile, 0, unroll=8)

    pl.semaphore_wait(barrier, greeted)
    copies = []

    def send(source, target, sem, which, landed):
        copy = pltpu.make_async_remote_copy(
            src_ref=source, dst_ref=target, send_sem=send_sem.at[sem], recv_sem=recv_sem.at[landed],
            device_id=beside(*which), device_id_type=MESH)
        copy.start()
        copies.append(copy)

    head, tail = pl.ds(0, 8), pl.ds(pairs - 8, 8)
    up_slot = jnp.where(at_north, 0, pairs + 1)
    down_slot = jnp.where(at_south, pairs + 1, 0)
    up_corner = pl.ds(pl.multiple_of(jnp.where(at_north, 0, pairs + 8), 8), 8)
    down_corner = pl.ds(pl.multiple_of(jnp.where(at_south, pairs + 8, 0), 8), 8)
    up_sem, down_sem = jnp.where(at_north, 0, 1), jnp.where(at_south, 1, 0)
    send(west_out, east_in.at[pl.ds(8, pairs)], 0, (lat, lon, -1), 6)
    send(east_out, west_in.at[pl.ds(8, pairs)], 1, (lat, lon, 1), 7)
    send(tiles.at[1], tiles.at[up_slot], 2, (up_lat, up_lon, 0), up_sem)
    send(tiles.at[pairs], tiles.at[down_slot], 3, (down_lat, down_lon, 0), down_sem)
    send(west_out.at[head], east_in.at[up_corner], 4, (up_lat, up_lon, -1), 2 + up_sem)
    send(east_out.at[head], west_in.at[up_corner], 5, (up_lat, up_lon, 1), 4 + up_sem)
    send(west_out.at[tail], east_in.at[down_corner], 6, (down_lat, down_lon, -1), 2 + down_sem)
    send(east_out.at[tail], west_in.at[down_corner], 7, (down_lat, down_lon, 1), 4 + down_sem)

    row = lax.broadcasted_iota(jnp.int32, (64, 128), 0)

    def beside_tile(even, odd, west_row, east_row):
        return (jnp.where(row == 0, west_row, pltpu.roll(odd, 1, 0)), jnp.where(row == 63, east_row, pltpu.roll(even, 63, 0)))

    def place(i, w, low, high, value):
        def at(block):
            return pl.ds(pl.multiple_of(block * 64 + low, 16), high - low)

        patches[at(i + 1), 256 * w : 256 * w + 128] = value
        patches[at(i), 256 * w + 128 : 256 * w + 192] = value[:, :64]
        patches[at(i + 2), 256 * w + 192 : 256 * w + 256] = value[:, 64:]

    def lay(i, carry):
        even, odd = tiles[i + 1, 0], tiles[i + 1, 1]
        west, east = beside_tile(even.astype(F32), odd.astype(F32), 0.0, 0.0)
        for w, value in enumerate((even, odd, west.astype(BF16), east.astype(BF16))):
            place(i, w, 0, 64, value)
        return carry

    lax.fori_loop(0, pairs, lay, 0, unroll=4)

    for load in loads[4:]:
        load.wait()

    def activate(n, carry):
        at = pl.ds(pl.multiple_of(n * 256, 256), 256)
        up = across(coarse_ref[at, :], tconv_ref[...])
        logistic = 0.5 * jnp.tanh(0.5 * up) + 0.5
        act_t[:, at] = (up * logistic).astype(BF16).T
        slope[at, :] = logistic * (1.0 + up * (1.0 - logistic))
        return carry

    lax.fori_loop(0, chunks, activate, 0, unroll=2)

    def block(tap):
        return conv_ref[:, 64 * tap : 64 * tap + 64]

    none = jnp.zeros((64, 64), BF16)
    places = {(s, w, h, p, q): t for s, w, h, p, q, t in window_blocks()}
    for s, w, h in [(s, w, h) for s in range(2) for w in range(4) for h in range(2)]:
        line = [block(places[s, w, h, p, q]) if (s, w, h, p, q) in places else none for p in range(2) for q in range(2)]
        at = w * 256 + s * 128 + h * 64
        weights[at : at + 64, :] = jnp.concatenate(line, axis=1)
    places = {(w, h, p, q): t for w, h, p, q, t in pole_blocks()}
    for w, h in [(w, h) for w in range(4) for h in range(2)]:
        line = [block(places[w, h, p, q]) if (w, h, p, q) in places else none for p in range(2) for q in range(2)]
        at = w * 128 + h * 64
        pole_weights[at : at + 64, :] = jnp.concatenate(line, axis=1)

    pole_extra[...] = jnp.zeros_like(pole_extra)
    pole_sums[...] = jnp.zeros_like(pole_sums)

    for landed, source in enumerate(
        (tiles.at[0], tiles.at[0], east_in.at[head], east_in.at[head], west_in.at[head],
         west_in.at[head], east_in.at[pl.ds(8, pairs)], west_in.at[pl.ds(8, pairs)])):
        pltpu.make_async_remote_copy(
            src_ref=source, dst_ref=source, send_sem=send_sem.at[0], recv_sem=recv_sem.at[landed],
            device_id=beside(lat, lon, 1), device_id_type=MESH).wait_recv()

    edge = lax.broadcasted_iota(jnp.int32, (16, 128), 0)

    def mend(i, carry):
        for w, low, at_row, halo in ((2, 0, 0, west_in), (3, 48, 15, east_in)):
            block = patches[pl.ds(pl.multiple_of((i + 1) * 64 + low, 16), 16), 256 * w : 256 * w + 128].astype(F32)
            block = jnp.where(edge == at_row, halo[pl.ds(i + 8, 1), :], block).astype(BF16)
            place(i, w, low, low + 16, block)
        return carry

    lax.fori_loop(0, pairs, mend, 0, unroll=4)

    def halo_windows(slot, corner):
        even, odd = tiles[slot, 0].astype(F32), tiles[slot, 1].astype(F32)
        return (even, odd) + beside_tile(even, odd, west_in[pl.ds(corner, 1), :], east_in[pl.ds(corner, 1), :])

    north = halo_windows(0, jnp.where(at_north, 0, 7))
    south = halo_windows(pairs + 1, jnp.where(at_south, pairs + 15, pairs + 8))
    last = pairs * 64
    for w in range(4):
        patches[64:128, 256 * w + 192 : 256 * w + 256] = jnp.where(at_north, 0.0, north[w][:, 64:]).astype(BF16)
        patches[last : last + 64, 256 * w + 128 : 256 * w + 192] = jnp.where(at_south, 0.0, south[w][:, :64]).astype(BF16)

    lane = lax.broadcasted_iota(jnp.int32, (64, 128), 1)
    blank = jnp.zeros((64, 128), BF16)

    @pl.when(at_north)
    def _():
        for w in range(4):
            pole_patches[:64, 128 * w : 128 * w + 128] = jnp.where(lane < 64, north[w], 0.0).astype(BF16)
            pole_patches[64:, 128 * w : 128 * w + 128] = blank
        pole_extra[0] = times(pole_patches[...], pole_weights[...])
        pole_sums[...] = times(act_t[:, :128], pole_patches[...])

    @pl.when(at_south)
    def _():
        for w in range(4):
            pole_patches[:64, 128 * w : 128 * w + 128] = blank
            pole_patches[64:, 128 * w : 128 * w + 128] = jnp.where(lane < 64, 0.0, south[w]).astype(BF16)
        pole_extra[1] = times(pole_patches[...], pole_weights[...])
        pole_sums[...] = times(act_t[:, last - 128 :], pole_patches[...])

    for n in range(chunks):
        at = slice(n * 256, n * 256 + 256)
        grad = times(patches[n * 256 + 64 : n * 256 + 320, :], weights[...])
        if n == 0:
            grad = jnp.concatenate([grad[:128] + pole_extra[0], grad[128:]], axis=0)
        if n == chunks - 1:
            grad = jnp.concatenate([grad[:128], grad[128:] + pole_extra[1]], axis=0)
        rounded = (grad * slope[at, :]).astype(BF16)
        pre[at, :] = rounded
        pre_t[:, at] = rounded.T
    members = shares.shape[1]
    share = 256 // members
    spare = 16 // members
    taps_grad = times(pre_t[...], coarse_ref[...])
    for m in range(members):
        shares[1, m, :share] = taps_grad[share * m : share * m + share]

    found = {}

    def add(tap, value):
        found[tap] = value if tap not in found else found[tap] + value

    for w in range(4):
        grads = times(act_t[...], patches[64 : last + 64, 256 * w : 256 * w + 256])
        for s, ww, h, p, q, t in window_blocks():
            if ww == w:
                at, col = 128 * p + 64 * q, s * 128 + h * 64
                add(t, grads[at : at + 64, col : col + 64])
    for w, h, p, q, t in pole_blocks():
        at, col = 128 * p + 64 * q, w * 128 + h * 64
        add(t, pole_sums[at : at + 64, col : col + 64])
    for b in range(4):
        both = jnp.concatenate([found[2 * b], found[2 * b + 1]], axis=0).T
        for m in range(members):
            low, high = max(64 * b, share * m), min(64 * b + 64, share * m + share)
            if low < high:
                shares[0, m, low - share * m : high - share * m] = both[low - 64 * b : high - 64 * b]
    last_tap = found[8].T
    last_tap = jnp.concatenate([last_tap[:32], last_tap[32:]], axis=1)
    for m in range(members):
        for core in range(2):
            at = 16 * core + spare * m
            shares[core, m, share:] = last_tap[at : at + spare]
    total.start()

    for n in range(chunks):
        at = slice(n * 256, n * 256 + 256)
        out_ref[at, :] = times(pre[at, :], tconv_ref[...]).astype(BF16)
    total.scatter()
    total.pass_on()
    total.give_back()
    total.bring_home()
    for copy in copies:
        copy.wait_send()
    total.end()
    for m in range(members):
        taps_out[share * m : share * m + share, :] = final[1, m, :share]
        for low in range(share * m, share * m + share, min(share, 64)):
            high, b = low + min(share, 64), low // 64
            conv_out[low - 64 * b : high - 64 * b, 128 * b : 128 * b + 128] = final[0, m, low - share * m : high - share * m]
        for core in range(2):
            at = 16 * core + spare * m
            line = final[core, m, share:]
            conv_out[at : at + spare, 512:] = line[:, :64]
            conv_out[32 + at : 32 + at + spare, 512:] = line[:, 64:]


def deliver_kernel(*refs):
    copies = [pltpu.make_async_copy(refs[n], refs[3 + n], refs[6].at[n]) for n in range(3)]
    for copy in copies:
        copy.start()
    for copy in copies:
        copy.wait()


def section(scale, coarse, cotangent, tconv, conv):
    cells = coarse.shape[0]
    pairs = cells // 64
    members, length = 2 * lax.axis_size("lat"), lax.axis_size("lon") // 4
    chunk = 272 // members
    vmem, hbm = pl.BlockSpec(memory_space=pltpu.VMEM), pl.BlockSpec(memory_space=pltpu.HBM)
    results = pl.pallas_call(
        functools.partial(section_kernel, scale),
        out_shape=(pltpu.VMEM((cells, 128), BF16), pltpu.VMEM((256, 128), F32), pltpu.VMEM(conv.shape, F32)),
        in_specs=[hbm] * 4,
        out_specs=(vmem, vmem, vmem),
        scratch_shapes=[
            pltpu.VMEM(coarse.shape, BF16), pltpu.VMEM(cotangent.shape, BF16), pltpu.VMEM(tconv.shape, BF16),
            pltpu.VMEM(conv.shape, BF16),
            pltpu.VMEM((cells * 2, 128), F32),
            pltpu.VMEM((pairs + 2, 2, 64, 128), BF16),
            pltpu.VMEM((pairs, 128), F32), pltpu.VMEM((pairs, 128), F32),
            pltpu.VMEM((pairs + 16, 128), F32), pltpu.VMEM((pairs + 16, 128), F32),
            pltpu.VMEM((cells + 128, 1024), BF16),
            pltpu.VMEM((256, cells), BF16),
            pltpu.VMEM((cells, 256), F32),
            pltpu.VMEM((cells, 256), BF16),
            pltpu.VMEM((256, cells), BF16),
            pltpu.VMEM((1024, 256), BF16),
            pltpu.VMEM((512, 256), BF16),
            pltpu.VMEM((128, 512), BF16),
            pltpu.VMEM((2, 128, 256), F32),
            pltpu.VMEM((256, 512), F32),
            pltpu.SemaphoreType.DMA((8,)), pltpu.SemaphoreType.DMA((8,)), pltpu.SemaphoreType.DMA((7,)),
            pltpu.VMEM((2, members, chunk, 128), F32),
            pltpu.VMEM((members, chunk, 128), F32), pltpu.VMEM((members, chunk, 128), F32),
            pltpu.VMEM((members, chunk, 128), F32), pltpu.VMEM((length, chunk, 128), F32),
            pltpu.VMEM((2, members, chunk, 128), F32),
            pltpu.SemaphoreType.DMA((5,)), pltpu.SemaphoreType.DMA((5,)),
        ],
        compiler_params=pltpu.CompilerParams(collective_id=0, has_side_effects=True, vmem_limit_bytes=VMEM_LIMIT),
        name="section",
    )(*(pltpu.with_memory_space_constraint(x, pltpu.HBM) for x in (coarse, cotangent, tconv, conv)))
    return pl.pallas_call(
        deliver_kernel,
        out_shape=tuple(pltpu.HBM(x.shape, x.dtype) for x in results),
        in_specs=[vmem] * 3,
        out_specs=(hbm,) * 3,
        scratch_shapes=[pltpu.SemaphoreType.DMA((3,))],
        name="deliver",
    )(*(pltpu.with_memory_space_constraint(x, pltpu.VMEM) for x in results))


def per_device(coarse_field, cotangent, tconv_weight, conv_weight):
    batch, channels, rows_here, cols_here = cotangent.shape
    in_channels = coarse_field.shape[1]
    coarse = coarse_field.transpose(0, 2, 3, 1).reshape(-1, in_channels)
    total_cells = batch * rows_here * cols_here * lax.axis_size("lat") * lax.axis_size("lon")
    coarse_grad, tconv_grad, conv_grad = section(
        1.0 / math.sqrt(total_cells), coarse, cotangent.reshape(channels * rows_here, cols_here),
        tconv_weight.reshape(4 * channels, in_channels), conv_weight)
    coarse_grad = coarse_grad.reshape(batch, rows_here // 2, cols_here // 2, in_channels).transpose(0, 3, 1, 2)
    return coarse_grad, tconv_grad.reshape(4, channels, in_channels), conv_grad


def solution(mesh):
    return jax.shard_map(
        per_device,
        mesh=mesh,
        in_specs=(P(None, None, "lat", "lon"), P(None, None, "lat", "lon"), P(), P()),
        out_specs=(P(None, None, "lat", "lon"), P(), P()),
        check_vma=False,
    )
```

```python
import functools
import math

import jax
import jax.numpy as jnp
from jax import lax
from jax.experimental import pallas as pl
from jax.experimental.pallas import tpu as pltpu
from jax.sharding import PartitionSpec as P

MESH = pl.DeviceIdType.MESH
F32, BF16 = jnp.float32, jnp.bfloat16
OWN, BESIDE = 0, 1
VMEM_LIMIT = 48 * 2**20


def row_step(source, half, p):
    step = p - half if source == OWN else (p - 2 if half == 0 else p + 1)
    return step if abs(step) <= 1 else None


def col_step(window, q):
    step = (q, q - 1, q + 1, q - 2)[window]
    return step if abs(step) <= 1 else None


def window_blocks():
    for source in (OWN, BESIDE):
        for window in range(4):
            for half in range(2):
                for p in range(2):
                    for q in range(2):
                        a, b = row_step(source, half, p), col_step(window, q)
                        if a is not None and b is not None:
                            yield source, window, half, p, q, 3 * (a + 1) + b + 1


def halo_blocks(side, polar):
    half = side if polar else 1 - side
    step = (2 * side - 1) if polar else (1 - 2 * side)
    for window in range(4):
        for q in range(2):
            b = col_step(window, q)
            if b is not None:
                yield window, half, side, q, 3 * (step + 1) + b + 1


def across(a, b):
    return lax.dot_general(a, b, (((1,), (1,)), ((), ())), preferred_element_type=F32)


def times(a, b):
    return jnp.dot(a, b, preferred_element_type=F32)


class Sum:
    def __init__(self, source, half, arrived, seen, along, final, scale, send, recv):
        self.source, self.half, self.arrived, self.seen, self.along, self.final = source, half, arrived, seen, along, final
        self.scale, self.send, self.recv = scale, send, recv
        self.lat, lon = lax.axis_index("lat"), lax.axis_index("lon")
        self.lats, lons = lax.axis_size("lat"), lax.axis_size("lon")
        self.side = lons // 2
        self.members, self.length = 2 * self.lats, lons // 4
        self.far = jnp.where(lon >= self.side, 1, 0)
        self.near = lon - self.far * self.side
        self.z, self.core = self.near // 2, self.near % 2
        self.mine = self.far * self.lats + self.lat
        self.far_first = sorted(
            range(1, self.members),
            key=lambda d: abs(2 * (d % self.lats) - self.lats) - 4 * (d // self.lats))

    def other(self):
        return {"lat": self.lat, "lon": self.far * self.side + self.z * 2 + 1 - self.core}

    def member(self, d):
        lat = self.lat + d % self.lats
        return jnp.where(lat >= self.lats, lat - self.lats, lat), (1 - self.far if d >= self.lats else self.far)

    def plane(self, d):
        lat, far = self.member(d)
        return {"lat": lat, "lon": far * self.side + self.near}

    def line(self, e):
        z = self.z + e
        z = jnp.where(z >= self.length, z - self.length, z)
        return {"lat": self.lat, "lon": self.far * self.side + z * 2 + self.core}

    def copy(self, source, target, phase, where):
        return pltpu.make_async_remote_copy(
            src_ref=source, dst_ref=target, send_sem=self.send.at[phase], recv_sem=self.recv.at[phase], device_id=where,
            device_id_type=MESH)

    def greet(self, barrier):
        def signal(peer):
            pl.semaphore_signal(barrier, inc=1, device_id=peer, device_id_type=MESH)

        signal(self.other())
        for d in self.far_first:
            signal(self.plane(d))
        for e in range(1, self.length):
            signal(self.line(e))
        return self.members + self.length - 1

    def all_of(self, phase):
        part = (self.arrived, self.seen.at[pl.ds(1, self.members - 1)], self.along.at[pl.ds(1, self.length - 1)],
                self.seen.at[pl.ds(1, self.members - 1)], self.arrived)[phase]
        return self.copy(part, part, phase, self.other())

    def start(self):
        self.copy(self.source.at[1 - self.core], self.arrived, 0, self.other()).start()

    def scatter(self):
        self.all_of(0).wait_recv()
        self.half[...] = self.source[self.core] + self.arrived[...]

        def send(d):
            lat, far = self.member(d)
            self.copy(self.half.at[far * self.lats + lat], self.seen.at[d], 1, self.plane(d)).start()

        for d in self.far_first:
            send(d)

    def pass_on(self):
        self.all_of(1).wait_recv()
        total = self.half[self.mine]
        for d in range(1, self.members):
            total = total + self.seen[d]
        self.along[self.z] = total
        for e in sorted(range(1, self.length), key=lambda e: abs(2 * e - self.length)):
            self.copy(self.along.at[self.z], self.along.at[self.z], 2, self.line(e)).start()

    def give_back(self):
        self.all_of(2).wait_recv()
        total = self.along[0]
        for z in range(1, self.length):
            total = total + self.along[z]
        self.final[self.core, self.mine] = total * self.scale
        at = self.final.at[self.core, self.mine]
        for d in self.far_first:
            self.copy(at, at, 3, self.plane(d)).start()

    def bring_home(self):
        self.all_of(3).wait_recv()
        self.copy(self.final.at[self.core], self.final.at[self.core], 4, self.other()).start()

    def end(self):
        self.all_of(4).wait_recv()
        for phase in range(5):
            self.all_of(phase).wait_send()


def section_kernel(
    scale, coarse_hbm, cot_hbm, tconv_hbm, conv_hbm, out_ref, taps_out, conv_out,
    coarse_ref, cot_ref, tconv_ref, conv_ref,
    spread, tiles, west_out, east_out, west_in, east_in, patches, act_t, slope, pre, pre_t, weights, half_grad, half_sums, halo_weights,
    halo_patches, send_sem, recv_sem, load_sem,
    shares, half, arrived, seen, along, final, sum_send, sum_recv,
):
    pairs = coarse_ref.shape[0] // 64
    chunks = pairs // 4
    loads = []
    quarter = cot_ref.shape[0] // 4
    for n in range(4):
        at = pl.ds(n * quarter, quarter)
        loads.append(pltpu.make_async_copy(cot_hbm.at[at], cot_ref.at[at], load_sem.at[n]))
    for n, (source, target) in enumerate(((coarse_hbm, coarse_ref), (tconv_hbm, tconv_ref), (conv_hbm, conv_ref))):
        loads.append(pltpu.make_async_copy(source, target, load_sem.at[4 + n]))
    for load in loads:
        load.start()

    lat, lon = lax.axis_index("lat"), lax.axis_index("lon")
    lats, lons = lax.axis_size("lat"), lax.axis_size("lon")
    at_north, at_south = lat == 0, lat == lats - 1
    opposite = lax.rem(lon + lons // 2, lons)
    up_lat, up_lon = jnp.where(at_north, 0, lat - 1), jnp.where(at_north, opposite, lon)
    down_lat, down_lon = jnp.where(at_south, lats - 1, lat + 1), jnp.where(at_south, opposite, lon)

    def beside(which_lat, which_lon, by):
        return {"lat": which_lat, "lon": lax.rem(which_lon + by + lons, lons)}

    total = Sum(shares, half, arrived, seen, along, final, scale, sum_send, sum_recv)

    barrier = pltpu.get_barrier_semaphore()
    greeted = 8 + total.greet(barrier)
    for which in ((lat, lon, -1), (lat, lon, 1), (up_lat, up_lon, -1), (up_lat, up_lon, 0), (up_lat, up_lon, 1),
                  (down_lat, down_lon, -1), (down_lat, down_lon, 0), (down_lat, down_lon, 1)):
        pl.semaphore_signal(barrier, inc=1, device_id=beside(*which), device_id_type=MESH)

    rows, cols = lax.broadcasted_iota(jnp.int32, (128, 128), 0), lax.broadcasted_iota(jnp.int32, (128, 128), 1)
    order = jnp.where(rows == (cols % 64) * 2 + cols // 64, 1.0, 0.0).astype(BF16)
    height = 2 * pairs

    def reorder(n, carry):
        at = pl.ds(pl.multiple_of(n * 512, 512), 512)
        spread[at, :] = times(cot_ref[at, :], order)
        return carry

    for n in range(4):
        loads[n].wait()
        lax.fori_loop(n * (quarter // 512), (n + 1) * (quarter // 512), reorder, 0, unroll=True)

    def make_tile(i, carry):
        pair = jnp.concatenate(
            [spread[pl.ds(2 * i, 64, stride=height), :], spread[pl.ds(2 * i + 1, 64, stride=height), :]], axis=0)
        tile = pair.astype(BF16).T
        tiles[i + 1, 0] = tile[:64]
        tiles[i + 1, 1] = tile[64:]
        west_out[pl.ds(i, 1), :] = tile[:16].astype(F32)[:1]
        east_out[pl.ds(i, 1), :] = tile[112:].astype(F32)[15:]
        return carry

    lax.fori_loop(0, pairs, make_tile, 0, unroll=8)

    pl.semaphore_wait(barrier, greeted)
    copies = []

    def send(source, target, sem, which, landed):
        copy = pltpu.make_async_remote_copy(
            src_ref=source, dst_ref=target, send_sem=send_sem.at[sem], recv_sem=recv_sem.at[landed],
            device_id=beside(*which), device_id_type=MESH)
        copy.start()
        copies.append(copy)

    head, tail = pl.ds(0, 8), pl.ds(pairs - 8, 8)
    up_slot = jnp.where(at_north, 0, pairs + 1)
    down_slot = jnp.where(at_south, pairs + 1, 0)
    up_corner = pl.ds(pl.multiple_of(jnp.where(at_north, 0, pairs + 8), 8), 8)
    down_corner = pl.ds(pl.multiple_of(jnp.where(at_south, pairs + 8, 0), 8), 8)
    up_sem, down_sem = jnp.where(at_north, 0, 1), jnp.where(at_south, 1, 0)
    send(west_out, east_in.at[pl.ds(8, pairs)], 0, (lat, lon, -1), 6)
    send(east_out, west_in.at[pl.ds(8, pairs)], 1, (lat, lon, 1), 7)
    send(tiles.at[1], tiles.at[up_slot], 2, (up_lat, up_lon, 0), up_sem)
    send(tiles.at[pairs], tiles.at[down_slot], 3, (down_lat, down_lon, 0), down_sem)
    send(west_out.at[head], east_in.at[up_corner], 4, (up_lat, up_lon, -1), 2 + up_sem)
    send(east_out.at[head], west_in.at[up_corner], 5, (up_lat, up_lon, 1), 4 + up_sem)
    send(west_out.at[tail], east_in.at[down_corner], 6, (down_lat, down_lon, -1), 2 + down_sem)
    send(east_out.at[tail], west_in.at[down_corner], 7, (down_lat, down_lon, 1), 4 + down_sem)

    row = lax.broadcasted_iota(jnp.int32, (64, 128), 0)

    def beside_tile(even, odd, west_row, east_row):
        return (jnp.where(row == 0, west_row, pltpu.roll(odd, 1, 0)), jnp.where(row == 63, east_row, pltpu.roll(even, 63, 0)))

    def place(i, w, low, high, value):
        def at(block):
            return pl.ds(pl.multiple_of(block * 64 + low, 16), high - low)

        patches[at(i + 1), 256 * w : 256 * w + 128] = value
        patches[at(i), 256 * w + 128 : 256 * w + 192] = value[:, :64]
        patches[at(i + 2), 256 * w + 192 : 256 * w + 256] = value[:, 64:]

    def lay(i, carry):
        even, odd = tiles[i + 1, 0], tiles[i + 1, 1]
        west, east = beside_tile(even.astype(F32), odd.astype(F32), 0.0, 0.0)
        for w, value in enumerate((even, odd, west.astype(BF16), east.astype(BF16))):
            place(i, w, 0, 64, value)
        return carry

    lax.fori_loop(0, pairs, lay, 0, unroll=4)
    for w in range(4):
        patches[64:128, 256 * w + 192 : 256 * w + 256] = jnp.zeros((64, 64), BF16)
        patches[pairs * 64 : pairs * 64 + 64, 256 * w + 128 : 256 * w + 192] = jnp.zeros((64, 64), BF16)

    for load in loads[4:]:
        load.wait()

    def activate(n, carry):
        at = pl.ds(pl.multiple_of(n * 256, 256), 256)
        up = across(coarse_ref[at, :], tconv_ref[...])
        logistic = 0.5 * jnp.tanh(0.5 * up) + 0.5
        act_t[:, at] = (up * logistic).astype(BF16).T
        slope[at, :] = logistic * (1.0 + up * (1.0 - logistic))
        return carry

    lax.fori_loop(0, chunks, activate, 0, unroll=2)

    def block(tap):
        return conv_ref[:, 64 * tap : 64 * tap + 64]

    none = jnp.zeros((64, 64), BF16)
    places = {(s, w, h, p, q): t for s, w, h, p, q, t in window_blocks()}
    for s, w, h in [(s, w, h) for s in range(2) for w in range(4) for h in range(2)]:
        line = [block(places[s, w, h, p, q]) if (s, w, h, p, q) in places else none for p in range(2) for q in range(2)]
        at = w * 256 + s * 128 + h * 64
        weights[at : at + 64, :] = jnp.concatenate(line, axis=1)
    def weigh_halo(side, polar):
        places = {(w, h, p, q): t for w, h, p, q, t in halo_blocks(side, polar)}
        for w, h in [(w, h) for w in range(4) for h in range(2)]:
            line = [block(places[w, h, p, q]) if (w, h, p, q) in places else none for p in range(2) for q in range(2)]
            at = w * 128 + h * 64
            halo_weights[side, at : at + 64, :] = jnp.concatenate(line, axis=1)

    at_pole = (at_north, at_south)
    for side in range(2):
        pl.when(at_pole[side])(lambda side=side: weigh_halo(side, True))
        pl.when(jnp.logical_not(at_pole[side]))(lambda side=side: weigh_halo(side, False))
    halo_patches[...] = jnp.zeros_like(halo_patches)

    last = pairs * 64
    for n in range(chunks):
        half_grad[n * 256 : n * 256 + 256, :] = times(patches[n * 256 + 64 : n * 256 + 320, :512], weights[:512, :])
    for w in range(2):
        half_sums[w] = times(act_t[...], patches[64 : last + 64, 256 * w : 256 * w + 256])

    for landed, source in enumerate(
        (tiles.at[0], tiles.at[0], east_in.at[head], east_in.at[head], west_in.at[head],
         west_in.at[head], east_in.at[pl.ds(8, pairs)], west_in.at[pl.ds(8, pairs)])):
        pltpu.make_async_remote_copy(
            src_ref=source, dst_ref=source, send_sem=send_sem.at[0], recv_sem=recv_sem.at[landed],
            device_id=beside(lat, lon, 1), device_id_type=MESH).wait_recv()

    edge = lax.broadcasted_iota(jnp.int32, (16, 128), 0)

    def mend(i, carry):
        for w, low, at_row, halo in ((2, 0, 0, west_in), (3, 48, 15, east_in)):
            block = patches[pl.ds(pl.multiple_of((i + 1) * 64 + low, 16), 16), 256 * w : 256 * w + 128].astype(F32)
            block = jnp.where(edge == at_row, halo[pl.ds(i + 8, 1), :], block).astype(BF16)
            place(i, w, low, low + 16, block)
        return carry

    lax.fori_loop(0, pairs, mend, 0, unroll=4)

    def halo_windows(slot, corner):
        even, odd = tiles[slot, 0].astype(F32), tiles[slot, 1].astype(F32)
        return (even, odd) + beside_tile(even, odd, west_in[pl.ds(corner, 1), :], east_in[pl.ds(corner, 1), :])

    north = halo_windows(0, jnp.where(at_north, 0, 7))
    south = halo_windows(pairs + 1, jnp.where(at_south, pairs + 15, pairs + 8))
    for w in range(4):
        halo_patches[0, :64, 128 * w : 128 * w + 128] = north[w].astype(BF16)
        halo_patches[1, 64:, 128 * w : 128 * w + 128] = south[w].astype(BF16)

    for n in range(chunks):
        at = slice(n * 256, n * 256 + 256)
        grad = half_grad[at, :] + times(patches[n * 256 + 64 : n * 256 + 320, 512:], weights[512:, :])
        if n == 0:
            grad = jnp.concatenate([grad[:128] + times(halo_patches[0], halo_weights[0]), grad[128:]], axis=0)
        if n == chunks - 1:
            grad = jnp.concatenate([grad[:128], grad[128:] + times(halo_patches[1], halo_weights[1])], axis=0)
        rounded = (grad * slope[at, :]).astype(BF16)
        pre[at, :] = rounded
        pre_t[:, at] = rounded.T
    members = shares.shape[1]
    share = 256 // members
    spare = 16 // members
    taps_grad = times(pre_t[...], coarse_ref[...])
    for m in range(members):
        shares[1, m, :share] = taps_grad[share * m : share * m + share]

    found = {}

    def add(tap, value):
        found[tap] = value if tap not in found else found[tap] + value

    for w in range(4):
        grads = half_sums[w] if w < 2 else times(act_t[...], patches[64 : last + 64, 256 * w : 256 * w + 256])
        for s, ww, h, p, q, t in window_blocks():
            if ww == w:
                at, col = 128 * p + 64 * q, s * 128 + h * 64
                add(t, grads[at : at + 64, col : col + 64])
    for side, cells in ((0, slice(0, 128)), (1, slice(last - 128, last))):
        grads = times(act_t[:, cells], halo_patches[side])
        for polar in (False, True):
            for w, h, p, q, t in halo_blocks(side, polar):
                at, col = 128 * p + 64 * q, w * 128 + h * 64
                part = grads[at : at + 64, col : col + 64]
                add(t, jnp.where(at_pole[side], part, 0.0) if polar else jnp.where(at_pole[side], 0.0, part))
    for b in range(4):
        both = jnp.concatenate([found[2 * b], found[2 * b + 1]], axis=0).T
        for m in range(members):
            low, high = max(64 * b, share * m), min(64 * b + 64, share * m + share)
            if low < high:
                shares[0, m, low - share * m : high - share * m] = both[low - 64 * b : high - 64 * b]
    last_tap = found[8].T
    last_tap = jnp.concatenate([last_tap[:32], last_tap[32:]], axis=1)
    for m in range(members):
        for core in range(2):
            at = 16 * core + spare * m
            shares[core, m, share:] = last_tap[at : at + spare]
    total.start()

    for n in range(chunks):
        at = slice(n * 256, n * 256 + 256)
        out_ref[at, :] = times(pre[at, :], tconv_ref[...]).astype(BF16)
    total.scatter()
    total.pass_on()
    total.give_back()
    total.bring_home()
    for copy in copies:
        copy.wait_send()
    total.end()
    for m in range(members):
        taps_out[share * m : share * m + share, :] = final[1, m, :share]
        for low in range(share * m, share * m + share, min(share, 64)):
            high, b = low + min(share, 64), low // 64
            conv_out[low - 64 * b : high - 64 * b, 128 * b : 128 * b + 128] = final[0, m, low - share * m : high - share * m]
        for core in range(2):
            at = 16 * core + spare * m
            line = final[core, m, share:]
            conv_out[at : at + spare, 512:] = line[:, :64]
            conv_out[32 + at : 32 + at + spare, 512:] = line[:, 64:]


def deliver_kernel(*refs):
    copies = [pltpu.make_async_copy(refs[n], refs[3 + n], refs[6].at[n]) for n in range(3)]
    for copy in copies:
        copy.start()
    for copy in copies:
        copy.wait()


def section(scale, coarse, cotangent, tconv, conv):
    cells = coarse.shape[0]
    pairs = cells // 64
    members, length = 2 * lax.axis_size("lat"), lax.axis_size("lon") // 4
    chunk = 272 // members
    vmem, hbm = pl.BlockSpec(memory_space=pltpu.VMEM), pl.BlockSpec(memory_space=pltpu.HBM)
    results = pl.pallas_call(
        functools.partial(section_kernel, scale),
        out_shape=(pltpu.VMEM((cells, 128), BF16), pltpu.VMEM((256, 128), F32), pltpu.VMEM(conv.shape, F32)),
        in_specs=[hbm] * 4,
        out_specs=(vmem, vmem, vmem),
        scratch_shapes=[
            pltpu.VMEM(coarse.shape, BF16), pltpu.VMEM(cotangent.shape, BF16), pltpu.VMEM(tconv.shape, BF16),
            pltpu.VMEM(conv.shape, BF16),
            pltpu.VMEM((cells * 2, 128), F32),
            pltpu.VMEM((pairs + 2, 2, 64, 128), BF16),
            pltpu.VMEM((pairs, 128), F32), pltpu.VMEM((pairs, 128), F32),
            pltpu.VMEM((pairs + 16, 128), F32), pltpu.VMEM((pairs + 16, 128), F32),
            pltpu.VMEM((cells + 128, 1024), BF16),
            pltpu.VMEM((256, cells), BF16),
            pltpu.VMEM((cells, 256), F32),
            pltpu.VMEM((cells, 256), BF16),
            pltpu.VMEM((256, cells), BF16),
            pltpu.VMEM((1024, 256), BF16),
            pltpu.VMEM((cells, 256), F32),
            pltpu.VMEM((2, 256, 256), F32),
            pltpu.VMEM((2, 512, 256), BF16),
            pltpu.VMEM((2, 128, 512), BF16),
            pltpu.SemaphoreType.DMA((8,)), pltpu.SemaphoreType.DMA((8,)), pltpu.SemaphoreType.DMA((7,)),
            pltpu.VMEM((2, members, chunk, 128), F32),
            pltpu.VMEM((members, chunk, 128), F32), pltpu.VMEM((members, chunk, 128), F32),
            pltpu.VMEM((members, chunk, 128), F32), pltpu.VMEM((length, chunk, 128), F32),
            pltpu.VMEM((2, members, chunk, 128), F32),
            pltpu.SemaphoreType.DMA((5,)), pltpu.SemaphoreType.DMA((5,)),
        ],
        compiler_params=pltpu.CompilerParams(collective_id=0, has_side_effects=True, vmem_limit_bytes=VMEM_LIMIT),
        name="section",
    )(*(pltpu.with_memory_space_constraint(x, pltpu.HBM) for x in (coarse, cotangent, tconv, conv)))
    return pl.pallas_call(
        deliver_kernel,
        out_shape=tuple(pltpu.HBM(x.shape, x.dtype) for x in results),
        in_specs=[vmem] * 3,
        out_specs=(hbm,) * 3,
        scratch_shapes=[pltpu.SemaphoreType.DMA((3,))],
        name="deliver",
    )(*(pltpu.with_memory_space_constraint(x, pltpu.VMEM) for x in results))


def per_device(coarse_field, cotangent, tconv_weight, conv_weight):
    batch, channels, rows_here, cols_here = cotangent.shape
    in_channels = coarse_field.shape[1]
    coarse = coarse_field.transpose(0, 2, 3, 1).reshape(-1, in_channels)
    total_cells = batch * rows_here * cols_here * lax.axis_size("lat") * lax.axis_size("lon")
    coarse_grad, tconv_grad, conv_grad = section(
        1.0 / math.sqrt(total_cells), coarse, cotangent.reshape(channels * rows_here, cols_here),
        tconv_weight.reshape(4 * channels, in_channels), conv_weight)
    coarse_grad = coarse_grad.reshape(batch, rows_here // 2, cols_here // 2, in_channels).transpose(0, 3, 1, 2)
    return coarse_grad, tconv_grad.reshape(4, channels, in_channels), conv_grad


def solution(mesh):
    return jax.shard_map(
        per_device,
        mesh=mesh,
        in_specs=(P(None, None, "lat", "lon"), P(None, None, "lat", "lon"), P(), P()),
        out_specs=(P(None, None, "lat", "lon"), P(), P()),
        check_vma=False,
    )
```

```python
import functools
import math

import jax
import jax.numpy as jnp
from jax import lax
from jax.experimental import pallas as pl
from jax.experimental.pallas import tpu as pltpu
from jax.sharding import PartitionSpec as P

MESH = pl.DeviceIdType.MESH
F32, BF16 = jnp.float32, jnp.bfloat16
OWN, BESIDE = 0, 1
VMEM_LIMIT = 48 * 2**20


def row_step(source, half, p):
    step = p - half if source == OWN else (p - 2 if half == 0 else p + 1)
    return step if abs(step) <= 1 else None


def col_step(window, q):
    step = (q, q - 1, q + 1, q - 2)[window]
    return step if abs(step) <= 1 else None


def window_blocks():
    for source in (OWN, BESIDE):
        for window in range(4):
            for half in range(2):
                for p in range(2):
                    for q in range(2):
                        a, b = row_step(source, half, p), col_step(window, q)
                        if a is not None and b is not None:
                            yield source, window, half, p, q, 3 * (a + 1) + b + 1


def halo_blocks(side, polar):
    half = side if polar else 1 - side
    step = (2 * side - 1) if polar else (1 - 2 * side)
    for window in range(4):
        for q in range(2):
            b = col_step(window, q)
            if b is not None:
                yield window, half, side, q, 3 * (step + 1) + b + 1


def across(a, b):
    return lax.dot_general(a, b, (((1,), (1,)), ((), ())), preferred_element_type=F32)


def times(a, b):
    return jnp.dot(a, b, preferred_element_type=F32)


class Sum:
    def __init__(self, source, half, arrived, seen, along, final, scale, send, recv):
        self.source, self.half, self.arrived, self.seen, self.along, self.final = source, half, arrived, seen, along, final
        self.scale, self.send, self.recv = scale, send, recv
        self.lat, lon = lax.axis_index("lat"), lax.axis_index("lon")
        self.lats, lons = lax.axis_size("lat"), lax.axis_size("lon")
        self.side = lons // 2
        self.members, self.length = 2 * self.lats, lons // 4
        self.far = jnp.where(lon >= self.side, 1, 0)
        self.near = lon - self.far * self.side
        self.z, self.core = self.near // 2, self.near % 2
        self.mine = self.far * self.lats + self.lat
        self.far_first = sorted(
            range(1, self.members),
            key=lambda d: abs(2 * (d % self.lats) - self.lats) - 4 * (d // self.lats))
        self.both_cores = [(turn, d) for d in self.far_first for turn in range(2)] + [(1, 0)]

    def other(self):
        return {"lat": self.lat, "lon": self.far * self.side + self.z * 2 + 1 - self.core}

    def member(self, d):
        lat = self.lat + d % self.lats
        return jnp.where(lat >= self.lats, lat - self.lats, lat), (1 - self.far if d >= self.lats else self.far)

    def plane(self, d, turn=0):
        lat, far = self.member(d)
        core = 1 - self.core if turn else self.core
        return {"lat": lat, "lon": far * self.side + self.z * 2 + core}

    def line(self, e):
        z = self.z + e
        z = jnp.where(z >= self.length, z - self.length, z)
        return {"lat": self.lat, "lon": self.far * self.side + z * 2 + self.core}

    def copy(self, source, target, phase, where):
        return pltpu.make_async_remote_copy(
            src_ref=source, dst_ref=target, send_sem=self.send.at[phase], recv_sem=self.recv.at[phase], device_id=where,
            device_id_type=MESH)

    def greet(self, barrier):
        def signal(peer):
            pl.semaphore_signal(barrier, inc=1, device_id=peer, device_id_type=MESH)

        for turn, d in self.both_cores:
            signal(self.plane(d, turn))
        for e in range(1, self.length):
            signal(self.line(e))
        return 2 * self.members + self.length - 2

    def all_of(self, phase):
        part = (self.arrived, self.seen.at[pl.ds(1, 2 * self.members - 1)], self.along.at[pl.ds(1, self.length - 1)],
                self.seen.at[pl.ds(1, 2 * self.members - 1)], self.arrived)[phase]
        return self.copy(part, part, phase, self.other())

    def scatter(self):
        for turn, d in self.both_cores:
            lat, far = self.member(d)
            core = 1 - self.core if turn else self.core
            self.copy(self.source.at[core, far * self.lats + lat], self.seen.at[turn * self.members + d], 1,
                      self.plane(d, turn)).start()

    def pass_on(self):
        self.all_of(1).wait_recv()
        total = self.source[self.core, self.mine]
        for d in range(1, 2 * self.members):
            total = total + self.seen[d]
        self.along[self.z] = total
        for e in sorted(range(1, self.length), key=lambda e: abs(2 * e - self.length)):
            self.copy(self.along.at[self.z], self.along.at[self.z], 2, self.line(e)).start()

    def give_back(self):
        self.all_of(2).wait_recv()
        total = self.along[0]
        for z in range(1, self.length):
            total = total + self.along[z]
        self.final[self.core, self.mine] = total * self.scale
        at = self.final.at[self.core, self.mine]
        for turn, d in self.both_cores:
            self.copy(at, at, 3, self.plane(d, turn)).start()

    def bring_home(self):
        self.all_of(3).wait_recv()

    def end(self):
        for phase in (1, 2, 3):
            self.all_of(phase).wait_send()


def section_kernel(
    scale, coarse_hbm, cot_hbm, tconv_hbm, conv_hbm, out_ref, taps_out, conv_out,
    coarse_ref, cot_ref, tconv_ref, conv_ref,
    spread, tiles, west_out, east_out, west_in, east_in, patches, act_t, slope, pre, pre_t, weights, half_grad, half_sums, halo_weights,
    halo_patches, send_sem, recv_sem, load_sem,
    shares, half, arrived, seen, along, final, sum_send, sum_recv,
):
    pairs = coarse_ref.shape[0] // 64
    chunks = pairs // 4
    loads = []
    quarter = cot_ref.shape[0] // 4
    for n in range(4):
        at = pl.ds(n * quarter, quarter)
        loads.append(pltpu.make_async_copy(cot_hbm.at[at], cot_ref.at[at], load_sem.at[n]))
    for n, (source, target) in enumerate(((coarse_hbm, coarse_ref), (tconv_hbm, tconv_ref), (conv_hbm, conv_ref))):
        loads.append(pltpu.make_async_copy(source, target, load_sem.at[4 + n]))
    for load in loads:
        load.start()

    lat, lon = lax.axis_index("lat"), lax.axis_index("lon")
    lats, lons = lax.axis_size("lat"), lax.axis_size("lon")
    at_north, at_south = lat == 0, lat == lats - 1
    opposite = lax.rem(lon + lons // 2, lons)
    up_lat, up_lon = jnp.where(at_north, 0, lat - 1), jnp.where(at_north, opposite, lon)
    down_lat, down_lon = jnp.where(at_south, lats - 1, lat + 1), jnp.where(at_south, opposite, lon)

    def beside(which_lat, which_lon, by):
        return {"lat": which_lat, "lon": lax.rem(which_lon + by + lons, lons)}

    total = Sum(shares, half, arrived, seen, along, final, scale, sum_send, sum_recv)

    barrier = pltpu.get_barrier_semaphore()
    greeted = 8 + total.greet(barrier)
    for which in ((lat, lon, -1), (lat, lon, 1), (up_lat, up_lon, -1), (up_lat, up_lon, 0), (up_lat, up_lon, 1),
                  (down_lat, down_lon, -1), (down_lat, down_lon, 0), (down_lat, down_lon, 1)):
        pl.semaphore_signal(barrier, inc=1, device_id=beside(*which), device_id_type=MESH)

    rows, cols = lax.broadcasted_iota(jnp.int32, (128, 128), 0), lax.broadcasted_iota(jnp.int32, (128, 128), 1)
    order = jnp.where(rows == (cols % 64) * 2 + cols // 64, 1.0, 0.0).astype(BF16)
    height = 2 * pairs

    def reorder(n, carry):
        at = pl.ds(pl.multiple_of(n * 512, 512), 512)
        spread[at, :] = times(cot_ref[at, :], order)
        return carry

    for n in range(4):
        loads[n].wait()
        lax.fori_loop(n * (quarter // 512), (n + 1) * (quarter // 512), reorder, 0, unroll=True)

    def make_tile(i, carry):
        pair = jnp.concatenate(
            [spread[pl.ds(2 * i, 64, stride=height), :], spread[pl.ds(2 * i + 1, 64, stride=height), :]], axis=0)
        tile = pair.astype(BF16).T
        tiles[i + 1, 0] = tile[:64]
        tiles[i + 1, 1] = tile[64:]
        west_out[pl.ds(i, 1), :] = tile[:16].astype(F32)[:1]
        east_out[pl.ds(i, 1), :] = tile[112:].astype(F32)[15:]
        return carry

    lax.fori_loop(0, pairs, make_tile, 0, unroll=8)

    pl.semaphore_wait(barrier, greeted)
    copies = []

    def send(source, target, sem, which, landed):
        copy = pltpu.make_async_remote_copy(
            src_ref=source, dst_ref=target, send_sem=send_sem.at[sem], recv_sem=recv_sem.at[landed],
            device_id=beside(*which), device_id_type=MESH)
        copy.start()
        copies.append(copy)

    head, tail = pl.ds(0, 8), pl.ds(pairs - 8, 8)
    up_slot = jnp.where(at_north, 0, pairs + 1)
    down_slot = jnp.where(at_south, pairs + 1, 0)
    up_corner = pl.ds(pl.multiple_of(jnp.where(at_north, 0, pairs + 8), 8), 8)
    down_corner = pl.ds(pl.multiple_of(jnp.where(at_south, pairs + 8, 0), 8), 8)
    up_sem, down_sem = jnp.where(at_north, 0, 1), jnp.where(at_south, 1, 0)
    send(west_out, east_in.at[pl.ds(8, pairs)], 0, (lat, lon, -1), 6)
    send(east_out, west_in.at[pl.ds(8, pairs)], 1, (lat, lon, 1), 7)
    send(tiles.at[1], tiles.at[up_slot], 2, (up_lat, up_lon, 0), up_sem)
    send(tiles.at[pairs], tiles.at[down_slot], 3, (down_lat, down_lon, 0), down_sem)
    send(west_out.at[head], east_in.at[up_corner], 4, (up_lat, up_lon, -1), 2 + up_sem)
    send(east_out.at[head], west_in.at[up_corner], 5, (up_lat, up_lon, 1), 4 + up_sem)
    send(west_out.at[tail], east_in.at[down_corner], 6, (down_lat, down_lon, -1), 2 + down_sem)
    send(east_out.at[tail], west_in.at[down_corner], 7, (down_lat, down_lon, 1), 4 + down_sem)

    row = lax.broadcasted_iota(jnp.int32, (64, 128), 0)

    def beside_tile(even, odd, west_row, east_row):
        return (jnp.where(row == 0, west_row, pltpu.roll(odd, 1, 0)), jnp.where(row == 63, east_row, pltpu.roll(even, 63, 0)))

    def place(i, w, low, high, value):
        def at(block):
            return pl.ds(pl.multiple_of(block * 64 + low, 16), high - low)

        patches[at(i + 1), 256 * w : 256 * w + 128] = value
        patches[at(i), 256 * w + 128 : 256 * w + 192] = value[:, :64]
        patches[at(i + 2), 256 * w + 192 : 256 * w + 256] = value[:, 64:]

    def lay(i, carry):
        even, odd = tiles[i + 1, 0], tiles[i + 1, 1]
        west, east = beside_tile(even.astype(F32), odd.astype(F32), 0.0, 0.0)
        for w, value in enumerate((even, odd, west.astype(BF16), east.astype(BF16))):
            place(i, w, 0, 64, value)
        return carry

    lax.fori_loop(0, pairs, lay, 0, unroll=4)
    for w in range(4):
        patches[64:128, 256 * w + 192 : 256 * w + 256] = jnp.zeros((64, 64), BF16)
        patches[pairs * 64 : pairs * 64 + 64, 256 * w + 128 : 256 * w + 192] = jnp.zeros((64, 64), BF16)

    for load in loads[4:]:
        load.wait()

    def activate(n, carry):
        at = pl.ds(pl.multiple_of(n * 256, 256), 256)
        up = across(coarse_ref[at, :], tconv_ref[...])
        logistic = 0.5 * jnp.tanh(0.5 * up) + 0.5
        act_t[:, at] = (up * logistic).astype(BF16).T
        slope[at, :] = logistic * (1.0 + up * (1.0 - logistic))
        return carry

    lax.fori_loop(0, chunks, activate, 0, unroll=2)

    def block(tap):
        return conv_ref[:, 64 * tap : 64 * tap + 64]

    none = jnp.zeros((64, 64), BF16)
    places = {(s, w, h, p, q): t for s, w, h, p, q, t in window_blocks()}
    for s, w, h in [(s, w, h) for s in range(2) for w in range(4) for h in range(2)]:
        line = [block(places[s, w, h, p, q]) if (s, w, h, p, q) in places else none for p in range(2) for q in range(2)]
        at = w * 256 + s * 128 + h * 64
        weights[at : at + 64, :] = jnp.concatenate(line, axis=1)
    def weigh_halo(side, polar):
        places = {(w, h, p, q): t for w, h, p, q, t in halo_blocks(side, polar)}
        for w, h in [(w, h) for w in range(4) for h in range(2)]:
            line = [block(places[w, h, p, q]) if (w, h, p, q) in places else none for p in range(2) for q in range(2)]
            at = w * 128 + h * 64
            halo_weights[side, at : at + 64, :] = jnp.concatenate(line, axis=1)

    at_pole = (at_north, at_south)
    for side in range(2):
        pl.when(at_pole[side])(lambda side=side: weigh_halo(side, True))
        pl.when(jnp.logical_not(at_pole[side]))(lambda side=side: weigh_halo(side, False))
    halo_patches[...] = jnp.zeros_like(halo_patches)

    last = pairs * 64
    for n in range(chunks):
        half_grad[n * 256 : n * 256 + 256, :] = times(patches[n * 256 + 64 : n * 256 + 320, :512], weights[:512, :])
    for w in range(2):
        half_sums[w] = times(act_t[...], patches[64 : last + 64, 256 * w : 256 * w + 256])

    for landed, source in enumerate(
        (tiles.at[0], tiles.at[0], east_in.at[head], east_in.at[head], west_in.at[head],
         west_in.at[head], east_in.at[pl.ds(8, pairs)], west_in.at[pl.ds(8, pairs)])):
        pltpu.make_async_remote_copy(
            src_ref=source, dst_ref=source, send_sem=send_sem.at[0], recv_sem=recv_sem.at[landed],
            device_id=beside(lat, lon, 1), device_id_type=MESH).wait_recv()

    edge = lax.broadcasted_iota(jnp.int32, (16, 128), 0)

    def mend(i, carry):
        for w, low, at_row, halo in ((2, 0, 0, west_in), (3, 48, 15, east_in)):
            block = patches[pl.ds(pl.multiple_of((i + 1) * 64 + low, 16), 16), 256 * w : 256 * w + 128].astype(F32)
            block = jnp.where(edge == at_row, halo[pl.ds(i + 8, 1), :], block).astype(BF16)
            place(i, w, low, low + 16, block)
        return carry

    lax.fori_loop(0, pairs, mend, 0, unroll=4)

    def halo_windows(slot, corner):
        even, odd = tiles[slot, 0].astype(F32), tiles[slot, 1].astype(F32)
        return (even, odd) + beside_tile(even, odd, west_in[pl.ds(corner, 1), :], east_in[pl.ds(corner, 1), :])

    north = halo_windows(0, jnp.where(at_north, 0, 7))
    south = halo_windows(pairs + 1, jnp.where(at_south, pairs + 15, pairs + 8))
    for w in range(4):
        halo_patches[0, :64, 128 * w : 128 * w + 128] = north[w].astype(BF16)
        halo_patches[1, 64:, 128 * w : 128 * w + 128] = south[w].astype(BF16)

    for n in range(chunks):
        at = slice(n * 256, n * 256 + 256)
        grad = half_grad[at, :] + times(patches[n * 256 + 64 : n * 256 + 320, 512:], weights[512:, :])
        if n == 0:
            grad = jnp.concatenate([grad[:128] + times(halo_patches[0], halo_weights[0]), grad[128:]], axis=0)
        if n == chunks - 1:
            grad = jnp.concatenate([grad[:128], grad[128:] + times(halo_patches[1], halo_weights[1])], axis=0)
        rounded = (grad * slope[at, :]).astype(BF16)
        pre[at, :] = rounded
        pre_t[:, at] = rounded.T
    members = shares.shape[1]
    share = 256 // members
    spare = 16 // members
    taps_grad = times(pre_t[...], coarse_ref[...])
    for m in range(members):
        shares[1, m, :share] = taps_grad[share * m : share * m + share]

    found = {}

    def add(tap, value):
        found[tap] = value if tap not in found else found[tap] + value

    for w in range(4):
        grads = half_sums[w] if w < 2 else times(act_t[...], patches[64 : last + 64, 256 * w : 256 * w + 256])
        for s, ww, h, p, q, t in window_blocks():
            if ww == w:
                at, col = 128 * p + 64 * q, s * 128 + h * 64
                add(t, grads[at : at + 64, col : col + 64])
    for side, cells in ((0, slice(0, 128)), (1, slice(last - 128, last))):
        grads = times(act_t[:, cells], halo_patches[side])
        for polar in (False, True):
            for w, h, p, q, t in halo_blocks(side, polar):
                at, col = 128 * p + 64 * q, w * 128 + h * 64
                part = grads[at : at + 64, col : col + 64]
                add(t, jnp.where(at_pole[side], part, 0.0) if polar else jnp.where(at_pole[side], 0.0, part))
    for b in range(4):
        both = jnp.concatenate([found[2 * b], found[2 * b + 1]], axis=0).T
        for m in range(members):
            low, high = max(64 * b, share * m), min(64 * b + 64, share * m + share)
            if low < high:
                shares[0, m, low - share * m : high - share * m] = both[low - 64 * b : high - 64 * b]
    last_tap = found[8].T
    last_tap = jnp.concatenate([last_tap[:32], last_tap[32:]], axis=1)
    for m in range(members):
        for core in range(2):
            at = 16 * core + spare * m
            shares[core, m, share:] = last_tap[at : at + spare]
    total.scatter()

    for n in range(chunks):
        at = slice(n * 256, n * 256 + 256)
        out_ref[at, :] = times(pre[at, :], tconv_ref[...]).astype(BF16)
    total.pass_on()
    total.give_back()
    total.bring_home()
    for copy in copies:
        copy.wait_send()
    total.end()
    for m in range(members):
        taps_out[share * m : share * m + share, :] = final[1, m, :share]
        for low in range(share * m, share * m + share, min(share, 64)):
            high, b = low + min(share, 64), low // 64
            conv_out[low - 64 * b : high - 64 * b, 128 * b : 128 * b + 128] = final[0, m, low - share * m : high - share * m]
        for core in range(2):
            at = 16 * core + spare * m
            line = final[core, m, share:]
            conv_out[at : at + spare, 512:] = line[:, :64]
            conv_out[32 + at : 32 + at + spare, 512:] = line[:, 64:]


def deliver_kernel(*refs):
    copies = [pltpu.make_async_copy(refs[n], refs[3 + n], refs[6].at[n]) for n in (1, 2)]
    quarter = refs[0].shape[0] // 4
    for n in range(4):
        at = pl.ds(n * quarter, quarter)
        copies.append(pltpu.make_async_copy(refs[0].at[at], refs[3].at[at], refs[6].at[3 + n]))
    for copy in copies:
        copy.start()
    for copy in copies:
        copy.wait()


def section(scale, coarse, cotangent, tconv, conv):
    cells = coarse.shape[0]
    pairs = cells // 64
    members, length = 2 * lax.axis_size("lat"), lax.axis_size("lon") // 4
    chunk = 272 // members
    vmem, hbm = pl.BlockSpec(memory_space=pltpu.VMEM), pl.BlockSpec(memory_space=pltpu.HBM)
    results = pl.pallas_call(
        functools.partial(section_kernel, scale),
        out_shape=(pltpu.VMEM((cells, 128), BF16), pltpu.VMEM((256, 128), F32), pltpu.VMEM(conv.shape, F32)),
        in_specs=[hbm] * 4,
        out_specs=(vmem, vmem, vmem),
        scratch_shapes=[
            pltpu.VMEM(coarse.shape, BF16), pltpu.VMEM(cotangent.shape, BF16), pltpu.VMEM(tconv.shape, BF16),
            pltpu.VMEM(conv.shape, BF16),
            pltpu.VMEM((cells * 2, 128), F32),
            pltpu.VMEM((pairs + 2, 2, 64, 128), BF16),
            pltpu.VMEM((pairs, 128), F32), pltpu.VMEM((pairs, 128), F32),
            pltpu.VMEM((pairs + 16, 128), F32), pltpu.VMEM((pairs + 16, 128), F32),
            pltpu.VMEM((cells + 128, 1024), BF16),
            pltpu.VMEM((256, cells), BF16),
            pltpu.VMEM((cells, 256), F32),
            pltpu.VMEM((cells, 256), BF16),
            pltpu.VMEM((256, cells), BF16),
            pltpu.VMEM((1024, 256), BF16),
            pltpu.VMEM((cells, 256), F32),
            pltpu.VMEM((2, 256, 256), F32),
            pltpu.VMEM((2, 512, 256), BF16),
            pltpu.VMEM((2, 128, 512), BF16),
            pltpu.SemaphoreType.DMA((8,)), pltpu.SemaphoreType.DMA((8,)), pltpu.SemaphoreType.DMA((7,)),
            pltpu.VMEM((2, members, chunk, 128), F32),
            pltpu.VMEM((members, chunk, 128), F32), pltpu.VMEM((members, chunk, 128), F32),
            pltpu.VMEM((2 * members, chunk, 128), F32), pltpu.VMEM((length, chunk, 128), F32),
            pltpu.VMEM((2, members, chunk, 128), F32),
            pltpu.SemaphoreType.DMA((5,)), pltpu.SemaphoreType.DMA((5,)),
        ],
        compiler_params=pltpu.CompilerParams(collective_id=0, has_side_effects=True, vmem_limit_bytes=VMEM_LIMIT),
        name="section",
    )(*(pltpu.with_memory_space_constraint(x, pltpu.HBM) for x in (coarse, cotangent, tconv, conv)))
    return pl.pallas_call(
        deliver_kernel,
        out_shape=tuple(pltpu.HBM(x.shape, x.dtype) for x in results),
        in_specs=[vmem] * 3,
        out_specs=(hbm,) * 3,
        scratch_shapes=[pltpu.SemaphoreType.DMA((7,))],
        name="deliver",
    )(*(pltpu.with_memory_space_constraint(x, pltpu.VMEM) for x in results))


def per_device(coarse_field, cotangent, tconv_weight, conv_weight):
    batch, channels, rows_here, cols_here = cotangent.shape
    in_channels = coarse_field.shape[1]
    coarse = coarse_field.transpose(0, 2, 3, 1).reshape(-1, in_channels)
    total_cells = batch * rows_here * cols_here * lax.axis_size("lat") * lax.axis_size("lon")
    coarse_grad, tconv_grad, conv_grad = section(
        1.0 / math.sqrt(total_cells), coarse, cotangent.reshape(channels * rows_here, cols_here),
        tconv_weight.reshape(4 * channels, in_channels), conv_weight)
    coarse_grad = coarse_grad.reshape(batch, rows_here // 2, cols_here // 2, in_channels).transpose(0, 3, 1, 2)
    return coarse_grad, tconv_grad.reshape(4, channels, in_channels), conv_grad


def solution(mesh):
    return jax.shard_map(
        per_device,
        mesh=mesh,
        in_specs=(P(None, None, "lat", "lon"), P(None, None, "lat", "lon"), P(), P()),
        out_specs=(P(None, None, "lat", "lon"), P(), P()),
        check_vma=False,
    )
```

```python
import functools
import math

import jax
import jax.numpy as jnp
from jax import lax
from jax.experimental import pallas as pl
from jax.experimental.pallas import tpu as pltpu
from jax.sharding import PartitionSpec as P

MESH = pl.DeviceIdType.MESH
F32, BF16 = jnp.float32, jnp.bfloat16
OWN, BESIDE = 0, 1
VMEM_LIMIT = 48 * 2**20


def row_step(source, half, p):
    step = p - half if source == OWN else (p - 2 if half == 0 else p + 1)
    return step if abs(step) <= 1 else None


def col_step(window, q):
    step = (q, q - 1, q + 1, q - 2)[window]
    return step if abs(step) <= 1 else None


def window_blocks():
    for source in (OWN, BESIDE):
        for window in range(4):
            for half in range(2):
                for p in range(2):
                    for q in range(2):
                        a, b = row_step(source, half, p), col_step(window, q)
                        if a is not None and b is not None:
                            yield source, window, half, p, q, 3 * (a + 1) + b + 1


def halo_blocks(side, polar):
    half = side if polar else 1 - side
    step = (2 * side - 1) if polar else (1 - 2 * side)
    for window in range(4):
        for q in range(2):
            b = col_step(window, q)
            if b is not None:
                yield window, half, side, q, 3 * (step + 1) + b + 1


def across(a, b):
    return lax.dot_general(a, b, (((1,), (1,)), ((), ())), preferred_element_type=F32)


def times(a, b):
    return jnp.dot(a, b, preferred_element_type=F32)


class Sum:
    def __init__(self, source, half, arrived, seen, along, final, scale, send, recv):
        self.source, self.half, self.arrived, self.seen, self.along, self.final = source, half, arrived, seen, along, final
        self.scale, self.send, self.recv = scale, send, recv
        self.lat, lon = lax.axis_index("lat"), lax.axis_index("lon")
        self.lats, lons = lax.axis_size("lat"), lax.axis_size("lon")
        self.side = lons // 2
        self.members, self.length = 2 * self.lats, lons // 4
        self.far = jnp.where(lon >= self.side, 1, 0)
        self.near = lon - self.far * self.side
        self.z, self.core = self.near // 2, self.near % 2
        self.mine = self.far * self.lats + self.lat
        self.far_first = sorted(
            range(1, self.members),
            key=lambda d: abs(2 * (d % self.lats) - self.lats) - 4 * (d // self.lats))
        self.both_cores = [(turn, d) for d in self.far_first for turn in range(2)] + [(1, 0)]

    def other(self):
        return {"lat": self.lat, "lon": self.far * self.side + self.z * 2 + 1 - self.core}

    def member(self, d):
        lat = self.lat + d % self.lats
        return jnp.where(lat >= self.lats, lat - self.lats, lat), (1 - self.far if d >= self.lats else self.far)

    def plane(self, d, turn=0):
        lat, far = self.member(d)
        core = 1 - self.core if turn else self.core
        return {"lat": lat, "lon": far * self.side + self.z * 2 + core}

    def line(self, e):
        z = self.z + e
        z = jnp.where(z >= self.length, z - self.length, z)
        return {"lat": self.lat, "lon": self.far * self.side + z * 2 + self.core}

    def copy(self, source, target, phase, where):
        return pltpu.make_async_remote_copy(
            src_ref=source, dst_ref=target, send_sem=self.send.at[phase], recv_sem=self.recv.at[phase], device_id=where,
            device_id_type=MESH)

    def greet(self, barrier):
        def signal(peer):
            pl.semaphore_signal(barrier, inc=1, device_id=peer, device_id_type=MESH)

        for turn, d in self.both_cores:
            signal(self.plane(d, turn))
        for e in range(1, self.length):
            signal(self.line(e))
        return 2 * self.members + self.length - 2

    def all_of(self, phase):
        part = (self.arrived, self.seen.at[pl.ds(1, 2 * self.members - 1)], self.along.at[pl.ds(1, self.length - 1)],
                self.seen.at[pl.ds(1, 2 * self.members - 1)], self.arrived)[phase]
        return self.copy(part, part, phase, self.other())

    def scatter(self):
        for turn, d in self.both_cores:
            lat, far = self.member(d)
            core = 1 - self.core if turn else self.core
            self.copy(self.source.at[core, far * self.lats + lat], self.seen.at[turn * self.members + d], 1,
                      self.plane(d, turn)).start()

    def pass_on(self):
        self.all_of(1).wait_recv()
        total = self.source[self.core, self.mine]
        for d in range(1, 2 * self.members):
            total = total + self.seen[d]
        self.along[self.z] = total
        for e in sorted(range(1, self.length), key=lambda e: abs(2 * e - self.length)):
            self.copy(self.along.at[self.z], self.along.at[self.z], 2, self.line(e)).start()

    def give_back(self):
        self.all_of(2).wait_recv()
        total = self.along[0]
        for z in range(1, self.length):
            total = total + self.along[z]
        self.final[self.core, self.mine] = total * self.scale
        at = self.final.at[self.core, self.mine]
        for turn, d in self.both_cores:
            self.copy(at, at, 3, self.plane(d, turn)).start()

    def bring_home(self):
        self.all_of(3).wait_recv()

    def end(self):
        for phase in (1, 2, 3):
            self.all_of(phase).wait_send()


def section_kernel(
    scale, coarse_hbm, cot_hbm, tconv_hbm, conv_hbm, out_ref, taps_out, conv_out,
    coarse_ref, cot_ref, tconv_ref, conv_ref,
    spread, tiles, west_out, east_out, west_in, east_in, patches, act_t, slope, pre, pre_t, weights, half_grad, half_sums, halo_weights,
    halo_patches, send_sem, recv_sem, load_sem,
    shares, half, arrived, seen, along, final, sum_send, sum_recv,
):
    pairs = coarse_ref.shape[0] // 64
    chunks = pairs // 4
    loads = []
    quarter = cot_ref.shape[0] // 4
    for n in range(4):
        at = pl.ds(n * quarter, quarter)
        loads.append(pltpu.make_async_copy(cot_hbm.at[at], cot_ref.at[at], load_sem.at[n]))
    for n, (source, target) in enumerate(((coarse_hbm, coarse_ref), (tconv_hbm, tconv_ref), (conv_hbm, conv_ref))):
        loads.append(pltpu.make_async_copy(source, target, load_sem.at[4 + n]))
    for load in loads:
        load.start()

    lat, lon = lax.axis_index("lat"), lax.axis_index("lon")
    lats, lons = lax.axis_size("lat"), lax.axis_size("lon")
    at_north, at_south = lat == 0, lat == lats - 1
    opposite = lax.rem(lon + lons // 2, lons)
    up_lat, up_lon = jnp.where(at_north, 0, lat - 1), jnp.where(at_north, opposite, lon)
    down_lat, down_lon = jnp.where(at_south, lats - 1, lat + 1), jnp.where(at_south, opposite, lon)

    def beside(which_lat, which_lon, by):
        return {"lat": which_lat, "lon": lax.rem(which_lon + by + lons, lons)}

    total = Sum(shares, half, arrived, seen, along, final, scale, sum_send, sum_recv)

    barrier = pltpu.get_barrier_semaphore()
    greeted = 8 + total.greet(barrier)
    for which in ((lat, lon, -1), (lat, lon, 1), (up_lat, up_lon, -1), (up_lat, up_lon, 0), (up_lat, up_lon, 1),
                  (down_lat, down_lon, -1), (down_lat, down_lon, 0), (down_lat, down_lon, 1)):
        pl.semaphore_signal(barrier, inc=1, device_id=beside(*which), device_id_type=MESH)

    rows, cols = lax.broadcasted_iota(jnp.int32, (128, 128), 0), lax.broadcasted_iota(jnp.int32, (128, 128), 1)
    order = jnp.where(rows == (cols % 64) * 2 + cols // 64, 1.0, 0.0).astype(BF16)
    height = 2 * pairs

    def reorder(n, carry):
        at = pl.ds(pl.multiple_of(n * 512, 512), 512)
        spread[at, :] = times(cot_ref[at, :], order)
        return carry

    for n in range(4):
        loads[n].wait()
        lax.fori_loop(n * (quarter // 512), (n + 1) * (quarter // 512), reorder, 0, unroll=True)

    def make_tile(i, carry):
        pair = jnp.concatenate(
            [spread[pl.ds(2 * i, 64, stride=height), :], spread[pl.ds(2 * i + 1, 64, stride=height), :]], axis=0)
        tile = pair.astype(BF16).T
        tiles[i + 1, 0] = tile[:64]
        tiles[i + 1, 1] = tile[64:]
        west_out[pl.ds(i, 1), :] = tile[:16].astype(F32)[:1]
        east_out[pl.ds(i, 1), :] = tile[112:].astype(F32)[15:]
        return carry

    lax.fori_loop(0, pairs, make_tile, 0, unroll=8)

    pl.semaphore_wait(barrier, greeted)
    copies = []

    def send(source, target, sem, which, landed):
        copy = pltpu.make_async_remote_copy(
            src_ref=source, dst_ref=target, send_sem=send_sem.at[sem], recv_sem=recv_sem.at[landed],
            device_id=beside(*which), device_id_type=MESH)
        copy.start()
        copies.append(copy)

    head, tail = pl.ds(0, 8), pl.ds(pairs - 8, 8)
    up_slot = jnp.where(at_north, 0, pairs + 1)
    down_slot = jnp.where(at_south, pairs + 1, 0)
    up_corner = pl.ds(pl.multiple_of(jnp.where(at_north, 0, pairs + 8), 8), 8)
    down_corner = pl.ds(pl.multiple_of(jnp.where(at_south, pairs + 8, 0), 8), 8)
    up_sem, down_sem = jnp.where(at_north, 0, 1), jnp.where(at_south, 1, 0)
    send(west_out, east_in.at[pl.ds(8, pairs)], 0, (lat, lon, -1), 6)
    send(east_out, west_in.at[pl.ds(8, pairs)], 1, (lat, lon, 1), 7)
    send(tiles.at[1], tiles.at[up_slot], 2, (up_lat, up_lon, 0), up_sem)
    send(tiles.at[pairs], tiles.at[down_slot], 3, (down_lat, down_lon, 0), down_sem)
    send(west_out.at[head], east_in.at[up_corner], 4, (up_lat, up_lon, -1), 2 + up_sem)
    send(east_out.at[head], west_in.at[up_corner], 5, (up_lat, up_lon, 1), 4 + up_sem)
    send(west_out.at[tail], east_in.at[down_corner], 6, (down_lat, down_lon, -1), 2 + down_sem)
    send(east_out.at[tail], west_in.at[down_corner], 7, (down_lat, down_lon, 1), 4 + down_sem)

    row = lax.broadcasted_iota(jnp.int32, (64, 128), 0)

    def beside_tile(even, odd, west_row, east_row):
        return (jnp.where(row == 0, west_row, pltpu.roll(odd, 1, 0)), jnp.where(row == 63, east_row, pltpu.roll(even, 63, 0)))

    def place(i, w, low, high, value):
        def at(block):
            return pl.ds(pl.multiple_of(block * 64 + low, 16), high - low)

        patches[at(i + 1), 256 * w : 256 * w + 128] = value
        patches[at(i), 256 * w + 128 : 256 * w + 192] = value[:, :64]
        patches[at(i + 2), 256 * w + 192 : 256 * w + 256] = value[:, 64:]

    def lay(i, carry):
        even, odd = tiles[i + 1, 0], tiles[i + 1, 1]
        west, east = beside_tile(even.astype(F32), odd.astype(F32), 0.0, 0.0)
        for w, value in enumerate((even, odd, west.astype(BF16), east.astype(BF16))):
            place(i, w, 0, 64, value)
        return carry

    lax.fori_loop(0, pairs, lay, 0, unroll=8)
    for w in range(4):
        patches[64:128, 256 * w + 192 : 256 * w + 256] = jnp.zeros((64, 64), BF16)
        patches[pairs * 64 : pairs * 64 + 64, 256 * w + 128 : 256 * w + 192] = jnp.zeros((64, 64), BF16)

    for load in loads[4:]:
        load.wait()

    def activate(n, carry):
        at = pl.ds(pl.multiple_of(n * 256, 256), 256)
        up = across(coarse_ref[at, :], tconv_ref[...])
        logistic = 0.5 * jnp.tanh(0.5 * up) + 0.5
        act_t[:, at] = (up * logistic).astype(BF16).T
        slope[at, :] = logistic * (1.0 + up * (1.0 - logistic))
        return carry

    lax.fori_loop(0, chunks, activate, 0, unroll=4)

    def block(tap):
        return conv_ref[:, 64 * tap : 64 * tap + 64]

    none = jnp.zeros((64, 64), BF16)
    places = {(s, w, h, p, q): t for s, w, h, p, q, t in window_blocks()}
    for s, w, h in [(s, w, h) for s in range(2) for w in range(4) for h in range(2)]:
        line = [block(places[s, w, h, p, q]) if (s, w, h, p, q) in places else none for p in range(2) for q in range(2)]
        at = w * 256 + s * 128 + h * 64
        weights[at : at + 64, :] = jnp.concatenate(line, axis=1)
    def weigh_halo(side, polar):
        places = {(w, h, p, q): t for w, h, p, q, t in halo_blocks(side, polar)}
        for w, h in [(w, h) for w in range(4) for h in range(2)]:
            line = [block(places[w, h, p, q]) if (w, h, p, q) in places else none for p in range(2) for q in range(2)]
            at = w * 128 + h * 64
            halo_weights[side, at : at + 64, :] = jnp.concatenate(line, axis=1)

    at_pole = (at_north, at_south)
    for side in range(2):
        pl.when(at_pole[side])(lambda side=side: weigh_halo(side, True))
        pl.when(jnp.logical_not(at_pole[side]))(lambda side=side: weigh_halo(side, False))
    halo_patches[...] = jnp.zeros_like(halo_patches)

    last = pairs * 64
    for n in range(chunks):
        half_grad[n * 256 : n * 256 + 256, :] = times(patches[n * 256 + 64 : n * 256 + 320, :512], weights[:512, :])
    for w in range(2):
        half_sums[w] = times(act_t[...], patches[64 : last + 64, 256 * w : 256 * w + 256])

    for landed, source in enumerate(
        (tiles.at[0], tiles.at[0], east_in.at[head], east_in.at[head], west_in.at[head],
         west_in.at[head], east_in.at[pl.ds(8, pairs)], west_in.at[pl.ds(8, pairs)])):
        pltpu.make_async_remote_copy(
            src_ref=source, dst_ref=source, send_sem=send_sem.at[0], recv_sem=recv_sem.at[landed],
            device_id=beside(lat, lon, 1), device_id_type=MESH).wait_recv()

    edge = lax.broadcasted_iota(jnp.int32, (16, 128), 0)

    def mend(i, carry):
        for w, low, at_row, halo in ((2, 0, 0, west_in), (3, 48, 15, east_in)):
            block = patches[pl.ds(pl.multiple_of((i + 1) * 64 + low, 16), 16), 256 * w : 256 * w + 128].astype(F32)
            block = jnp.where(edge == at_row, halo[pl.ds(i + 8, 1), :], block).astype(BF16)
            place(i, w, low, low + 16, block)
        return carry

    lax.fori_loop(0, pairs, mend, 0, unroll=16)

    def halo_windows(slot, corner):
        even, odd = tiles[slot, 0].astype(F32), tiles[slot, 1].astype(F32)
        return (even, odd) + beside_tile(even, odd, west_in[pl.ds(corner, 1), :], east_in[pl.ds(corner, 1), :])

    north = halo_windows(0, jnp.where(at_north, 0, 7))
    south = halo_windows(pairs + 1, jnp.where(at_south, pairs + 15, pairs + 8))
    for w in range(4):
        halo_patches[0, :64, 128 * w : 128 * w + 128] = north[w].astype(BF16)
        halo_patches[1, 64:, 128 * w : 128 * w + 128] = south[w].astype(BF16)

    for n in range(chunks):
        at = slice(n * 256, n * 256 + 256)
        grad = half_grad[at, :] + times(patches[n * 256 + 64 : n * 256 + 320, 512:], weights[512:, :])
        if n == 0:
            grad = jnp.concatenate([grad[:128] + times(halo_patches[0], halo_weights[0]), grad[128:]], axis=0)
        if n == chunks - 1:
            grad = jnp.concatenate([grad[:128], grad[128:] + times(halo_patches[1], halo_weights[1])], axis=0)
        rounded = (grad * slope[at, :]).astype(BF16)
        pre[at, :] = rounded
        pre_t[:, at] = rounded.T
    members = shares.shape[1]
    share = 256 // members
    spare = 16 // members
    taps_grad = times(pre_t[...], coarse_ref[...])
    for m in range(members):
        shares[1, m, :share] = taps_grad[share * m : share * m + share]

    found = {}

    def add(tap, value):
        found[tap] = value if tap not in found else found[tap] + value

    for w in range(4):
        grads = half_sums[w] if w < 2 else times(act_t[...], patches[64 : last + 64, 256 * w : 256 * w + 256])
        for s, ww, h, p, q, t in window_blocks():
            if ww == w:
                at, col = 128 * p + 64 * q, s * 128 + h * 64
                add(t, grads[at : at + 64, col : col + 64])
    for side, cells in ((0, slice(0, 128)), (1, slice(last - 128, last))):
        grads = times(act_t[:, cells], halo_patches[side])
        for polar in (False, True):
            for w, h, p, q, t in halo_blocks(side, polar):
                at, col = 128 * p + 64 * q, w * 128 + h * 64
                part = grads[at : at + 64, col : col + 64]
                add(t, jnp.where(at_pole[side], part, 0.0) if polar else jnp.where(at_pole[side], 0.0, part))
    for b in range(4):
        both = jnp.concatenate([found[2 * b], found[2 * b + 1]], axis=0).T
        for m in range(members):
            low, high = max(64 * b, share * m), min(64 * b + 64, share * m + share)
            if low < high:
                shares[0, m, low - share * m : high - share * m] = both[low - 64 * b : high - 64 * b]
    last_tap = found[8].T
    last_tap = jnp.concatenate([last_tap[:32], last_tap[32:]], axis=1)
    for m in range(members):
        for core in range(2):
            at = 16 * core + spare * m
            shares[core, m, share:] = last_tap[at : at + spare]
    total.scatter()

    for n in range(chunks):
        at = slice(n * 256, n * 256 + 256)
        out_ref[at, :] = times(pre[at, :], tconv_ref[...]).astype(BF16)
    total.pass_on()
    total.give_back()
    total.bring_home()
    for copy in copies:
        copy.wait_send()
    total.end()
    for m in range(members):
        taps_out[share * m : share * m + share, :] = final[1, m, :share]
        for low in range(share * m, share * m + share, min(share, 64)):
            high, b = low + min(share, 64), low // 64
            conv_out[low - 64 * b : high - 64 * b, 128 * b : 128 * b + 128] = final[0, m, low - share * m : high - share * m]
        for core in range(2):
            at = 16 * core + spare * m
            line = final[core, m, share:]
            conv_out[at : at + spare, 512:] = line[:, :64]
            conv_out[32 + at : 32 + at + spare, 512:] = line[:, 64:]


def deliver_kernel(*refs):
    copies = [pltpu.make_async_copy(refs[n], refs[3 + n], refs[6].at[n]) for n in (1, 2)]
    quarter = refs[0].shape[0] // 4
    for n in range(4):
        at = pl.ds(n * quarter, quarter)
        copies.append(pltpu.make_async_copy(refs[0].at[at], refs[3].at[at], refs[6].at[3 + n]))
    for copy in copies:
        copy.start()
    for copy in copies:
        copy.wait()


def section(scale, coarse, cotangent, tconv, conv):
    cells = coarse.shape[0]
    pairs = cells // 64
    members, length = 2 * lax.axis_size("lat"), lax.axis_size("lon") // 4
    chunk = 272 // members
    vmem, hbm = pl.BlockSpec(memory_space=pltpu.VMEM), pl.BlockSpec(memory_space=pltpu.HBM)
    results = pl.pallas_call(
        functools.partial(section_kernel, scale),
        out_shape=(pltpu.VMEM((cells, 128), BF16), pltpu.VMEM((256, 128), F32), pltpu.VMEM(conv.shape, F32)),
        in_specs=[hbm] * 4,
        out_specs=(vmem, vmem, vmem),
        scratch_shapes=[
            pltpu.VMEM(coarse.shape, BF16), pltpu.VMEM(cotangent.shape, BF16), pltpu.VMEM(tconv.shape, BF16),
            pltpu.VMEM(conv.shape, BF16),
            pltpu.VMEM((cells * 2, 128), F32),
            pltpu.VMEM((pairs + 2, 2, 64, 128), BF16),
            pltpu.VMEM((pairs, 128), F32), pltpu.VMEM((pairs, 128), F32),
            pltpu.VMEM((pairs + 16, 128), F32), pltpu.VMEM((pairs + 16, 128), F32),
            pltpu.VMEM((cells + 128, 1024), BF16),
            pltpu.VMEM((256, cells), BF16),
            pltpu.VMEM((cells, 256), F32),
            pltpu.VMEM((cells, 256), BF16),
            pltpu.VMEM((256, cells), BF16),
            pltpu.VMEM((1024, 256), BF16),
            pltpu.VMEM((cells, 256), F32),
            pltpu.VMEM((2, 256, 256), F32),
            pltpu.VMEM((2, 512, 256), BF16),
            pltpu.VMEM((2, 128, 512), BF16),
            pltpu.SemaphoreType.DMA((8,)), pltpu.SemaphoreType.DMA((8,)), pltpu.SemaphoreType.DMA((7,)),
            pltpu.VMEM((2, members, chunk, 128), F32),
            pltpu.VMEM((members, chunk, 128), F32), pltpu.VMEM((members, chunk, 128), F32),
            pltpu.VMEM((2 * members, chunk, 128), F32), pltpu.VMEM((length, chunk, 128), F32),
            pltpu.VMEM((2, members, chunk, 128), F32),
            pltpu.SemaphoreType.DMA((5,)), pltpu.SemaphoreType.DMA((5,)),
        ],
        compiler_params=pltpu.CompilerParams(collective_id=0, has_side_effects=True, vmem_limit_bytes=VMEM_LIMIT),
        name="section",
    )(*(pltpu.with_memory_space_constraint(x, pltpu.HBM) for x in (coarse, cotangent, tconv, conv)))
    return pl.pallas_call(
        deliver_kernel,
        out_shape=tuple(pltpu.HBM(x.shape, x.dtype) for x in results),
        in_specs=[vmem] * 3,
        out_specs=(hbm,) * 3,
        scratch_shapes=[pltpu.SemaphoreType.DMA((7,))],
        name="deliver",
    )(*(pltpu.with_memory_space_constraint(x, pltpu.VMEM) for x in results))


def per_device(coarse_field, cotangent, tconv_weight, conv_weight):
    batch, channels, rows_here, cols_here = cotangent.shape
    in_channels = coarse_field.shape[1]
    coarse = coarse_field.transpose(0, 2, 3, 1).reshape(-1, in_channels)
    total_cells = batch * rows_here * cols_here * lax.axis_size("lat") * lax.axis_size("lon")
    coarse_grad, tconv_grad, conv_grad = section(
        1.0 / math.sqrt(total_cells), coarse, cotangent.reshape(channels * rows_here, cols_here),
        tconv_weight.reshape(4 * channels, in_channels), conv_weight)
    coarse_grad = coarse_grad.reshape(batch, rows_here // 2, cols_here // 2, in_channels).transpose(0, 3, 1, 2)
    return coarse_grad, tconv_grad.reshape(4, channels, in_channels), conv_grad


def solution(mesh):
    return jax.shard_map(
        per_device,
        mesh=mesh,
        in_specs=(P(None, None, "lat", "lon"), P(None, None, "lat", "lon"), P(), P()),
        out_specs=(P(None, None, "lat", "lon"), P(), P()),
        check_vma=False,
    )
```
